32 devices in a mesh: sub: 4 (over y, x), row: 2 (over core), col: 4 (over z).
Axes of the slice: x: 2, y: 2, z: 4, core: 2. Of those that a mesh axis runs over, the one named last changes fastest.
Arguments:
- leaf_rhs: bfloat16 [4, 8, 4, 64, 256], P('sub', 'row', 'col'), may hold values from -6 to 6
- leaf_inverse: bfloat16 [4, 8, 4, 256, 256], P('sub', 'row', 'col'), may hold values from -0.5 to 0.5
- coupling: bfloat16 [4, 16, 8, 4, 256, 256], P('sub', 'row', None, 'col'), may hold values from -0.03125 to 0.03125
- pattern: int32 [4, 16, 8, 4], P('sub', 'row', None, 'col'), may hold values 0 or 1
- top_rhs: bfloat16 [16, 64, 256], replicated, may hold values from -6 to 6
- top_inverse: bfloat16 [16, 256, 256], replicated, may hold values from -0.5 to 0.5
- top_factor: bfloat16 [16, 16, 256, 256], P('row', 'col'), may hold values from -0.09375 to 0.09375
Outputs:
- leaf_solution: bfloat16 [4, 8, 4, 64, 256], P('sub', 'row', 'col')
- top_solution: bfloat16 [16, 64, 256], P('row')
The draws below stay inside these ranges and needn't reach their ends.
All inputs are finite; a program needn't handle non-finite values. No bound on the sum of `pattern` on one device may be relied on, other than what follows from the above.
Results may differ from the reference program's by a relative error of at most 0.025.
Values may be sent and summed in bfloat16 or wider, within the bound.
A program may use at most 128 MiB of HBM per device.

```python
import jax
import jax.numpy as jnp
from jax import lax

B = 256
NRHS = 64
KT = 16
SUBTREES = 4
LCOLS = 4
NLC = 8


def set_ends(array, rng, low, high):
    index_at = [jax.random.randint(jax.random.fold_in(rng, axis), (), 0, length) for axis, length in enumerate(array.shape)]
    widest = array.shape.index(max(array.shape))
    beside = index_at[:widest] + [(index_at[widest] + 1) % array.shape[widest]] + index_at[widest + 1:]
    return array.at[tuple(index_at)].set(low).at[tuple(beside)].set(high)


def levels(key, shape, pieces, smallest, largest):
    gain = 1.0
    for position, shards_of in pieces:
        draws = jax.random.uniform(jax.random.fold_in(jax.random.fold_in(key, 6), position), (shards_of,), jnp.float32, smallest / len(pieces), largest / len(pieces))
        gain = gain * jnp.repeat(jnp.exp(draws), shape[position] // shards_of).reshape((-1,) + (1,) * (len(shape) - 1 - position))
    return gain


def centred(key, dims, width, bound, pieces=(), dtype=jnp.bfloat16):
    result = jax.random.normal(key, dims, jnp.float32) * width
    if len(pieces) > 0:
        result = levels(key, dims, pieces, -0.22, 0.18) * result
    return jnp.clip(result, min=-bound, max=bound).astype(dtype)


def setup_inputs(seed: int = 0) -> dict:
    key_list = jax.random.split(jax.random.key(seed), 8)
    leaf_rhs = centred(key_list[0], (SUBTREES, NLC, LCOLS, NRHS, B), 1.0, 6.0, ((0, 4), (1, 2), (2, 4)))
    leaf_inverse = centred(key_list[1], (SUBTREES, NLC, LCOLS, B, B), (B // 2) ** -0.5, 0.5, ((0, 4), (1, 2), (2, 4)))
    coupling = centred(key_list[2], (SUBTREES, KT, NLC, LCOLS, B, B), (B * NLC * LCOLS * SUBTREES) ** -0.5, 0.03125, ((0, 4), (1, 2), (3, 4)))
    pattern = set_ends((jax.random.randint(key_list[3], (SUBTREES, KT, NLC, LCOLS), 0, 3) < 2).astype(jnp.int32), jax.random.fold_in(key_list[3], 1), 0, 1)
    top_rhs = centred(key_list[4], (KT, NRHS, B), 1.0, 6.0)
    top_inverse = centred(key_list[5], (KT, B, B), (B // 2) ** -0.5, 0.5)
    top_factor = centred(key_list[6], (KT, KT, B, B), (B * KT) ** -0.5, 0.09375, ((0, 2), (1, 4)))
    return {"leaf_rhs": leaf_rhs, "leaf_inverse": leaf_inverse, "coupling": coupling, "pattern": pattern, "top_rhs": top_rhs, "top_inverse": top_inverse, "top_factor": top_factor}


def reference(leaf_rhs, leaf_inverse, coupling, pattern, top_rhs, top_inverse, top_factor):
    leaf_tri = jnp.tril(leaf_inverse)
    leaf_forward = jnp.einsum('sicnb,sicdb->sicnd', leaf_rhs.astype(jnp.float32), leaf_tri.astype(jnp.float32)).astype(jnp.bfloat16)
    weights = pattern.astype(jnp.bfloat16)

    def updates_of(block_id):
        def one_subtree(sub_id):
            blocks = coupling[sub_id, block_id] * weights[sub_id, block_id][:, :, None, None]
            flat_left = jnp.transpose(leaf_forward[sub_id], (2, 0, 1, 3)).reshape(NRHS, -1)
            flat_right = jnp.transpose(blocks, (2, 0, 1, 3)).reshape(B, -1)
            return jnp.dot(flat_left, flat_right.T, preferred_element_type=jnp.float32)
        return jnp.sum(lax.map(one_subtree, jnp.arange(SUBTREES)), axis=0)

    updates = lax.map(updates_of, jnp.arange(KT))
    forward_rows = []
    for block_id in range(KT):
        summed = top_rhs[block_id].astype(jnp.float32) - updates[block_id]
        for earlier in range(block_id):
            summed = summed - jnp.dot(forward_rows[earlier], top_factor[block_id, earlier].T, preferred_element_type=jnp.float32)
        residue = summed.astype(jnp.bfloat16)
        forward_rows.append(jnp.dot(residue, jnp.tril(top_inverse[block_id]).T, preferred_element_type=jnp.float32).astype(jnp.bfloat16))
    solved_rows = [None] * KT
    for block_id in reversed(range(KT)):
        summed = forward_rows[block_id].astype(jnp.float32)
        for later in range(block_id + 1, KT):
            summed = summed - jnp.dot(solved_rows[later], top_factor[later, block_id], preferred_element_type=jnp.float32)
        residue = summed.astype(jnp.bfloat16)
        solved_rows[block_id] = jnp.dot(residue, jnp.tril(top_inverse[block_id]), preferred_element_type=jnp.float32).astype(jnp.bfloat16)
    top_solution = jnp.stack(solved_rows)
    flat_solution = jnp.transpose(top_solution, (1, 0, 2)).reshape(NRHS, KT * B)

    def back_of(sub_id):
        blocks = coupling[sub_id] * weights[sub_id][:, :, :, None, None]
        flat_blocks = jnp.transpose(blocks, (0, 3, 1, 2, 4)).reshape(KT * B, -1)
        product = jnp.dot(flat_solution, flat_blocks, preferred_element_type=jnp.float32)
        return jnp.transpose(product.reshape(NRHS, NLC, LCOLS, B), (1, 2, 0, 3))

    back_sums = lax.map(back_of, jnp.arange(SUBTREES))
    leaf_residue = (leaf_forward.astype(jnp.float32) - back_sums).astype(jnp.bfloat16)
    leaf_solution = jnp.einsum('sicnb,sicbd->sicnd', leaf_residue.astype(jnp.float32), leaf_tri.astype(jnp.float32)).astype(jnp.bfloat16)
    return leaf_solution, top_solution
```

```python
import functools

import jax
import jax.numpy as jnp
from jax import lax
from jax.experimental import pallas as pl
from jax.experimental.pallas import tpu as pltpu
from jax.sharding import PartitionSpec as P

BF = jnp.bfloat16
F32 = jnp.float32


def dot_nt(a, b):
    return lax.dot_general(a, b, (((1,), (1,)), ((), ())), preferred_element_type=F32)


def dot_nn(a, b):
    return lax.dot_general(a, b, (((1,), (0,)), ((), ())), preferred_element_type=F32)


def lower(block):
    rows = lax.broadcasted_iota(jnp.int32, block.shape, 0)
    cols = lax.broadcasted_iota(jnp.int32, block.shape, 1)
    return jnp.where(rows >= cols, block.astype(F32), 0.0).astype(BF)


def kernel(
    S, R, C,
    pat, rhs_h, linv_h, coup_h, trhs_h, tinv_h, tf_h,
    out, top_h,
    rhs, ginv, gt, coup, y, u, ub, d1, v, d2, tf, ti, tr, W, res, xf,
    fws, fwr, xs, bwr, x, acc, zb, zr,
    ld, cp_sem, y_ss, y_rs, tf_ss, tf_rs, d1_ss, d1_rs, d2_ss, d2_rs,
    fw_ss, fw_rs, bw_ss, bw_rs, x1_ss, x1_rs, x2_ss, x2_rs, z_ss, z_rs,
):
    s, r, c = lax.axis_index("sub"), lax.axis_index("row"), lax.axis_index("col")
    Kr, _, Ni, B, _ = coup.shape
    KT, Kc = tf.shape[:2]
    n = y.shape[2]
    ns = n // S
    Kg = min(Kr, Kc)
    chunks = Kr // Kg
    Q = Kc // Kg
    lead = (c * Kc) // Kr
    is_lead = r == lead
    mine = pl.ds(pl.multiple_of(s * ns, ns), ns)

    def remote(src, dst, ss, rs, dev):
        return pltpu.make_async_remote_copy(
            src_ref=src, dst_ref=dst, send_sem=ss, recv_sem=rs,
            device_id=dev, device_id_type=pl.DeviceIdType.MESH,
        )

    def group_of(j):
        return (r * Kr + j * Kg) // Kc

    loads = [
        pltpu.make_async_copy(linv_h, ginv, ld.at[0]),
        pltpu.make_async_copy(rhs_h, rhs, ld.at[1]),
    ]
    for cp in loads:
        cp.start()

    def coup_copy(a, p):
        rr = lax.rem(r + p, R)
        return pltpu.make_async_copy(coup_h.at[a, rr], coup.at[a, rr], cp_sem.at[a, p])

    for p in range(R):
        for a in range(Kr):
            coup_copy(a, p).start()
    ti_copy = pltpu.make_async_copy(tinv_h.at[pl.ds(c * Kc, Kc)], ti, ld.at[2])
    tr_copy = pltpu.make_async_copy(trhs_h.at[pl.ds(c * Kc, Kc), mine], tr, ld.at[3])
    tf_copy = pltpu.make_async_copy(tf_h, tf.at[pl.ds(r * Kr, Kr)], ld.at[4])

    @pl.when(is_lead)
    def _():
        ti_copy.start()
        tr_copy.start()
        tf_copy.start()

    barrier = pltpu.get_barrier_semaphore()
    for p in range(1, S):
        pl.semaphore_signal(
            barrier, inc=1, device_id=(lax.rem(s + p, S), r, c), device_id_type=pl.DeviceIdType.MESH
        )
    for p in range(R):
        for q in range(C):
            if p == 0 and q == 0:
                continue
            pl.semaphore_signal(
                barrier, inc=1, device_id=(s, lax.rem(r + p, R), lax.rem(c + q, C)),
                device_id_type=pl.DeviceIdType.MESH,
            )

    for cp in loads:
        cp.wait()
    for i in range(Ni):
        g = lower(ginv[i])
        gt[i] = g
        y[r, i] = dot_nt(rhs[i], g).astype(BF)

    pl.semaphore_wait(barrier, S - 1 + R * C - 1)

    def y_send(p):
        return remote(y.at[r], y.at[r], y_ss.at[p], y_rs.at[p], (s, lax.rem(r + p, R), c))

    def y_from(p):
        src = lax.rem(r + R - p, R)
        return remote(y.at[src], y.at[src], y_ss.at[p], y_rs.at[p], (s, src, c))

    for p in range(1, R):
        y_send(p).start()

    tf_send = remote(tf_h, tf.at[pl.ds(r * Kr, Kr)], tf_ss, tf_rs.at[r], (s, lead, c))

    @pl.when(r > lead)
    def _():
        tf_send.start()

    def tf_wait(rr):
        remote(tf_h, tf.at[pl.ds(rr * Kr, Kr)], tf_ss, tf_rs.at[rr], (s, lead, c)).wait_recv()

    def add(a, rr, first):
        total = None if first else u[a]
        for i in range(Ni):
            w = pat[a, rr * Ni + i].astype(F32)
            term = dot_nt(y[rr, i], coup[a, rr, i]) * w
            total = term if total is None else total + term
        return total

    def d1_send(j, p):
        to = lax.rem(s + p, S)
        rows = pl.ds(pl.multiple_of(to * ns, ns), ns)
        blocks = pl.ds(j * Kg, Kg)
        return remote(
            ub.at[blocks, rows], d1.at[p, blocks], d1_ss.at[j, p], d1_rs.at[j, p], (to, r, c)
        )

    for a in range(Kr):
        coup_copy(a, 0).wait()
        u[a] = add(a, r, True)
    for p in range(1, R):
        y_from(R - p).wait_recv()
        for a in range(Kr):
            coup_copy(a, p).wait()
            total = add(a, lax.rem(r + p, R), False)
            if p < R - 1:
                u[a] = total
            else:
                u[a] = total
                ub[a] = total.astype(BF)
                if a % Kg == Kg - 1:
                    for t in range(1, S):
                        d1_send(a // Kg, t).start()

    def d2_send(j):
        g = group_of(j)
        pos = lax.rem(r * Kr + j * Kg, Kc)
        return remote(
            v.at[pl.ds(j * Kg, Kg)], d2.at[c, pl.ds(pos, Kg)], d2_ss.at[j],
            d2_rs.at[pos // Kg, c], (s, (g * Kc) // Kr, g),
        )

    def self_lead(j):
        return jnp.logical_and(is_lead, group_of(j) == c)

    for j in range(chunks):
        for p in range(1, S):
            d1_send(j, p).wait_recv()
        for b in range(Kg):
            a = j * Kg + b
            total = u[a, mine, :]
            for p in range(1, S):
                total = total + d1[p, a].astype(F32)
            v[a] = total.astype(BF)

        @pl.when(self_lead(j))
        def _():
            d2[c, pl.ds(0, Kg)] = v[pl.ds(j * Kg, Kg)]

        @pl.when(jnp.logical_not(self_lead(j)))
        def _():
            d2_send(j).start()

    def blk(k):
        return pl.ds(k * B, B)

    def fw_copy(src_c, dst_c):
        return remote(
            fws.at[dst_c], fwr.at[src_c], fw_ss.at[dst_c], fw_rs.at[src_c],
            (s, (dst_c * Kc) // Kr, dst_c),
        )

    def bw_copy(src_c, dst_c):
        return remote(
            xs, bwr.at[src_c], bw_ss.at[dst_c], bw_rs.at[src_c],
            (s, (dst_c * Kc) // Kr, dst_c),
        )

    def x1_copy(q, to):
        owner = lead + q
        local = c * Kc + q * Kg - owner * Kr
        return remote(
            xs.at[pl.ds(q * Kg, Kg)], x.at[pl.ds(local, Kg), mine], x1_ss.at[q, to],
            x1_rs.at[local // Kg], (s, owner, to),
        )

    @pl.when(is_lead)
    def _():
        ti_copy.wait()
        tf_copy.wait()
        for q in range(1, Q):
            tf_wait(lead + q)
        base = c * Kc
        for k in range(Kc):
            g = lower(ti[k])
            W[blk(k), blk(k)] = g
            for b in range(k):
                t = None
                for m in range(b, k):
                    term = dot_nn(tf[base + k, m], W[blk(m), blk(b)])
                    t = term if t is None else t + term
                W[blk(k), blk(b)] = (-dot_nn(g, t.astype(BF))).astype(BF)
        tr_copy.wait()
        for q in range(Q):
            for o in range(C):
                def take(q=q, o=o):
                    remote(
                        v.at[pl.ds(0, Kg)], d2.at[o, pl.ds(q * Kg, Kg)], d2_ss.at[0],
                        d2_rs.at[q, o], (s, lead + q, o),
                    ).wait_recv()
                if q == 0:
                    pl.when(c != o)(take)
                else:
                    take()
        for k in range(Kc):
            total = tr[k].astype(F32)
            for o in range(C):
                total = total - d2[o, k].astype(F32)
            res[k] = total
        for o in range(C - 1):
            @pl.when(c > o)
            def _(o=o):
                fw_copy(o, c).wait_recv()
                for k in range(Kc):
                    res[k] = res[k] - fwr[o, k].astype(F32)
        rb = [res[k].astype(BF) for k in range(Kc)]
        fb = []
        for k in range(Kc):
            t = dot_nt(rb[k], W[blk(k), blk(k)])
            for b in range(k):
                t = t + dot_nt(rb[b], W[blk(k), blk(b)])
            fb.append(t.astype(BF))
            xf[k] = fb[k]
        for o in range(1, C):
            @pl.when(c < o)
            def _(o=o):
                for rr in range(R):
                    if (rr * Kr) // Kc == o:
                        tf_wait(rr)
                for k in range(Kc):
                    t = None
                    for b in range(Kc):
                        term = dot_nt(xf[b], tf[o * Kc + k, b])
                        t = term if t is None else t + term
                    fws[o, k] = t.astype(BF)
                fw_copy(c, o).start()
        for k in range(Kc):
            res[k] = xf[k].astype(F32)
        for o in range(C - 1, 0, -1):
            @pl.when(c < o)
            def _(o=o):
                bw_copy(o, c).wait_recv()
                for k in range(Kc):
                    t = res[k]
                    for a in range(Kc):
                        t = t - dot_nn(bwr[o, a], tf[o * Kc + a, k])
                    res[k] = t
        wb = [res[k].astype(BF) for k in range(Kc)]
        for k in range(Kc):
            t = dot_nn(wb[k], W[blk(k), blk(k)])
            for a in range(k + 1, Kc):
                t = t + dot_nn(wb[a], W[blk(a), blk(k)])
            xs[k] = t.astype(BF)
        for o in range(C - 2, -1, -1):
            @pl.when(c > o)
            def _(o=o):
                bw_copy(c, o).start()
        local = c * Kc - lead * Kr
        for b in range(Kg):
            x[local + b, mine, :] = xs[b]
        for q in range(Q):
            for o in range(C):
                if q == 0:
                    @pl.when(c != o)
                    def _(q=q, o=o):
                        x1_copy(q, o).start()
                else:
                    x1_copy(q, o).start()

    def x2_copy(j, p):
        place = x.at[pl.ds(j * Kg, Kg), mine]
        return remote(place, place, x2_ss.at[j, p], x2_rs.at[j, p], (lax.rem(s + p, S), r, c))

    def x2_from(j, p):
        src = lax.rem(s + S - p, S)
        place = x.at[pl.ds(j * Kg, Kg), pl.ds(pl.multiple_of(src * ns, ns), ns)]
        return remote(place, place, x2_ss.at[j, p], x2_rs.at[j, p], (src, r, c))

    def z_send(p):
        to = lax.rem(r + p, R)
        return remote(zb.at[p], zr.at[p], z_ss.at[p], z_rs.at[p], (s, to, c))

    for j in range(chunks - 1, -1, -1):
        @pl.when(jnp.logical_not(self_lead(j)))
        def _():
            place = x.at[pl.ds(j * Kg, Kg), mine]
            remote(place, place, x1_ss.at[0, 0], x1_rs.at[j], (s, r, c)).wait_recv()
        for p in range(1, S):
            x2_copy(j, p).start()
        for p in range(1, S):
            x2_from(j, p).wait_recv()
        if j == 0:
            top_copy = pltpu.make_async_copy(x, top_h, ld.at[5])
            top_copy.start()
        for p in [*range(1, R), 0]:
            rr = lax.rem(r + p, R)
            for i in range(Ni):
                t = None if j == chunks - 1 else acc[p, i]
                for b in range(Kg):
                    a = j * Kg + b
                    w = pat[a, rr * Ni + i].astype(F32)
                    term = dot_nn(x[a], coup[a, rr, i]) * w
                    t = term if t is None else t + term
                if j == 0 and p > 0:
                    zb[p, i] = t.astype(BF)
                else:
                    acc[p, i] = t
            if j == 0 and p > 0:
                z_send(p).start()

    for p in range(1, R):
        z_send(p).wait_recv()
    for i in range(Ni):
        t = y[r, i].astype(F32) - acc[0, i]
        for p in range(1, R):
            t = t - zr[p, i].astype(F32)
        out[i] = dot_nn(t.astype(BF), gt[i]).astype(BF)

    top_copy.wait()
    for p in range(1, R):
        y_send(p).wait_send()
        z_send(p).wait_send()

    @pl.when(r > lead)
    def _():
        tf_send.wait_send()

    for j in range(chunks):
        for p in range(1, S):
            d1_send(j, p).wait_send()
            x2_copy(j, p).wait_send()

        @pl.when(jnp.logical_not(self_lead(j)))
        def _():
            d2_send(j).wait_send()

    @pl.when(is_lead)
    def _():
        for o in range(C):
            @pl.when(c < o)
            def _(o=o):
                fw_copy(c, o).wait_send()

            @pl.when(c > o)
            def _(o=o):
                bw_copy(c, o).wait_send()
            for q in range(Q):
                if q == 0:
                    @pl.when(c != o)
                    def _(q=q, o=o):
                        x1_copy(q, o).wait_send()
                else:
                    x1_copy(q, o).wait_send()


def local(sizes, leaf_rhs, leaf_inverse, coupling, pattern, top_rhs, top_inverse, top_factor):
    S, R, C = sizes
    _, Kr, NL, _, B, _ = coupling.shape
    Ni = NL // R
    KT, n, _ = top_rhs.shape
    Kc = top_factor.shape[1]
    ns = n // S
    Kg = min(Kr, Kc)
    chunks, Q = Kr // Kg, Kc // Kg
    V = pltpu.VMEM
    D = pltpu.SemaphoreType.DMA
    any_spec = pl.BlockSpec(memory_space=pl.ANY)
    scratch = [
        V((Ni, n, B), BF), V((Ni, B, B), BF), V((Ni, B, B), BF),
        V((Kr, R, Ni, B, B), BF), V((R, Ni, n, B), BF),
        V((Kr, n, B), F32), V((Kr, n, B), BF), V((S, Kr, ns, B), BF), V((Kr, ns, B), BF),
        V((C, Kc, ns, B), BF), V((KT, Kc, B, B), BF), V((Kc, B, B), BF), V((Kc, ns, B), BF),
        V((Kc * B, Kc * B), BF), V((Kc, ns, B), F32), V((Kc, ns, B), BF),
        V((C, Kc, ns, B), BF), V((C, Kc, ns, B), BF), V((Kc, ns, B), BF), V((C, Kc, ns, B), BF),
        V((Kr, n, B), BF), V((R, Ni, n, B), F32), V((R, Ni, n, B), BF), V((R, Ni, n, B), BF),
        D((6,)), D((Kr, R)), D((R,)), D((R,)), D, D((R,)),
        D((chunks, S)), D((chunks, S)), D((chunks,)), D((Q, C)),
        D((C,)), D((C,)), D((C,)), D((C,)),
        D((Q, C)), D((chunks,)), D((chunks, S)), D((chunks, S)), D((R,)), D((R,)),
    ]
    leaf, top = pl.pallas_call(
        functools.partial(kernel, S, R, C),
        out_shape=(
            jax.ShapeDtypeStruct((Ni, n, B), BF),
            jax.ShapeDtypeStruct((Kr, n, B), BF),
        ),
        in_specs=[pl.BlockSpec(memory_space=pltpu.SMEM)] + [any_spec] * 6,
        out_specs=(pl.BlockSpec(memory_space=pltpu.VMEM), any_spec),
        scratch_shapes=scratch,
        compiler_params=pltpu.CompilerParams(
            collective_id=0, has_side_effects=True, vmem_limit_bytes=56 * 1024 * 1024
        ),
    )(
        pattern.reshape(Kr, NL),
        leaf_rhs.reshape(Ni, n, B),
        leaf_inverse.reshape(Ni, B, B),
        coupling.reshape(Kr, R, Ni, B, B),
        top_rhs,
        top_inverse,
        top_factor,
    )
    return leaf[None, :, None], top


def solution(mesh):
    placed = (
        P("sub", "row", "col", None, None),
        P("sub", "row", "col", None, None),
        P("sub", "row", None, "col", None, None),
        P("sub", "row", None, "col"),
        P(),
        P(),
        P("row", "col", None, None),
    )
    sizes = tuple(mesh.shape[name] for name in ("sub", "row", "col"))
    return jax.shard_map(
        functools.partial(local, sizes),
        mesh=mesh,
        in_specs=placed,
        out_specs=(P("sub", "row", "col", None, None), P("row", None, None)),
        check_vma=False,
    )
```

```python
import functools

import jax
import jax.numpy as jnp
from jax import lax
from jax.experimental import pallas as pl
from jax.experimental.pallas import tpu as pltpu
from jax.sharding import PartitionSpec as P

BF = jnp.bfloat16
F32 = jnp.float32


def dot_nt(a, b):
    return lax.dot_general(a, b, (((1,), (1,)), ((), ())), preferred_element_type=F32)


def dot_nn(a, b):
    return lax.dot_general(a, b, (((1,), (0,)), ((), ())), preferred_element_type=F32)


def lower(block):
    rows = lax.broadcasted_iota(jnp.int32, block.shape, 0)
    cols = lax.broadcasted_iota(jnp.int32, block.shape, 1)
    return jnp.where(rows >= cols, block.astype(F32), 0.0).astype(BF)


def kernel(
    S, R, C,
    pat, rhs_h, linv_h, coup_h, trhs_h, tinv_h, tf_h,
    out, top,
    rhs, ginv, gt, coup, y, u, ub, d1, v, d2, tf, ti, tr, W, res, xf,
    fws, fwr, xs, bwr, x, acc, zb, zr,
    ld, cp_sem, y_ss, y_rs, tf_ss, tf_rs, d1_ss, d1_rs, d2_ss, d2_rs,
    fw_ss, fw_rs, bw_ss, bw_rs, x1_ss, x1_rs, x2_ss, x2_rs, z_ss, z_rs,
):
    s, r, c = lax.axis_index("sub"), lax.axis_index("row"), lax.axis_index("col")
    Kr, _, Ni, B, _ = coup.shape
    KT, Kc = tf.shape[:2]
    n = y.shape[2]
    ns = n // S
    Kg = min(Kr, Kc)
    chunks = Kr // Kg
    Q = Kc // Kg
    lead = (c * Kc) // Kr
    is_lead = r == lead
    mine = pl.ds(pl.multiple_of(s * ns, ns), ns)

    def remote(src, dst, ss, rs, dev):
        return pltpu.make_async_remote_copy(
            src_ref=src, dst_ref=dst, send_sem=ss, recv_sem=rs,
            device_id=dev, device_id_type=pl.DeviceIdType.MESH,
        )

    def group_of(j):
        return (r * Kr + j * Kg) // Kc

    loads = [
        pltpu.make_async_copy(linv_h, ginv, ld.at[0]),
        pltpu.make_async_copy(rhs_h, rhs, ld.at[1]),
    ]
    for cp in loads:
        cp.start()

    def coup_copy(a, p):
        rr = lax.rem(r + p, R)
        return pltpu.make_async_copy(coup_h.at[a, rr], coup.at[a, rr], cp_sem.at[a, p])

    for p in range(R):
        for a in range(Kr):
            coup_copy(a, p).start()
    ti_copy = pltpu.make_async_copy(tinv_h.at[pl.ds(c * Kc, Kc)], ti, ld.at[2])
    tr_copy = pltpu.make_async_copy(trhs_h.at[pl.ds(c * Kc, Kc), mine], tr, ld.at[3])
    tf_copy = pltpu.make_async_copy(tf_h, tf.at[pl.ds(r * Kr, Kr)], ld.at[4])

    @pl.when(is_lead)
    def _():
        ti_copy.start()
        tr_copy.start()
        tf_copy.start()

    barrier = pltpu.get_barrier_semaphore()
    for p in range(1, S):
        pl.semaphore_signal(
            barrier, inc=1, device_id=(lax.rem(s + p, S), r, c), device_id_type=pl.DeviceIdType.MESH
        )
    for p in range(R):
        for q in range(C):
            if p == 0 and q == 0:
                continue
            pl.semaphore_signal(
                barrier, inc=1, device_id=(s, lax.rem(r + p, R), lax.rem(c + q, C)),
                device_id_type=pl.DeviceIdType.MESH,
            )

    for cp in loads:
        cp.wait()
    for i in range(Ni):
        g = lower(ginv[i])
        gt[i] = g
        y[r, i] = dot_nt(rhs[i], g).astype(BF)

    pl.semaphore_wait(barrier, S - 1 + R * C - 1)

    def y_send(p):
        return remote(y.at[r], y.at[r], y_ss.at[p], y_rs.at[p], (s, lax.rem(r + p, R), c))

    def y_from(p):
        src = lax.rem(r + R - p, R)
        return remote(y.at[src], y.at[src], y_ss.at[p], y_rs.at[p], (s, src, c))

    for p in range(1, R):
        y_send(p).start()

    tf_send = remote(tf_h, tf.at[pl.ds(r * Kr, Kr)], tf_ss, tf_rs.at[r], (s, lead, c))

    @pl.when(r > lead)
    def _():
        tf_send.start()

    def tf_wait(rr):
        remote(tf_h, tf.at[pl.ds(rr * Kr, Kr)], tf_ss, tf_rs.at[rr], (s, lead, c)).wait_recv()

    def add(a, rr, first):
        total = None if first else u[a]
        for i in range(Ni):
            w = pat[a, rr * Ni + i].astype(F32)
            term = dot_nt(y[rr, i], coup[a, rr, i]) * w
            total = term if total is None else total + term
        return total

    def d1_send(j, p):
        to = lax.rem(s + p, S)
        rows = pl.ds(pl.multiple_of(to * ns, ns), ns)
        blocks = pl.ds(j * Kg, Kg)
        return remote(
            ub.at[blocks, rows], d1.at[p, blocks], d1_ss.at[j, p], d1_rs.at[j, p], (to, r, c)
        )

    for a in range(Kr):
        coup_copy(a, 0).wait()
        u[a] = add(a, r, True)
    for p in range(1, R):
        y_from(R - p).wait_recv()
        for a in range(Kr):
            coup_copy(a, p).wait()
            total = add(a, lax.rem(r + p, R), False)
            if p < R - 1:
                u[a] = total
            else:
                u[a] = total
                ub[a] = total.astype(BF)
                if a % Kg == Kg - 1:
                    for t in range(1, S):
                        d1_send(a // Kg, t).start()

    def d2_send(j):
        g = group_of(j)
        pos = lax.rem(r * Kr + j * Kg, Kc)
        return remote(
            v.at[pl.ds(j * Kg, Kg)], d2.at[c, pl.ds(pos, Kg)], d2_ss.at[j],
            d2_rs.at[pos // Kg, c], (s, (g * Kc) // Kr, g),
        )

    def self_lead(j):
        return jnp.logical_and(is_lead, group_of(j) == c)

    def blk(k):
        return pl.ds(k * B, B)

    def w_row(k):
        g = lower(ti[k])
        W[blk(k), blk(k)] = g
        for b in range(k):
            t = None
            for m in range(b, k):
                term = dot_nn(tf[c * Kc + k, m], W[blk(m), blk(b)])
                t = term if t is None else t + term
            W[blk(k), blk(b)] = (-dot_nn(g, t.astype(BF))).astype(BF)

    @pl.when(is_lead)
    def _():
        ti_copy.wait()
        tf_copy.wait()
        for q in range(1, Q):
            tf_wait(lead + q)
        for k in range(Kc - 1):
            w_row(k)

    for j in range(chunks):
        for p in range(1, S):
            d1_send(j, p).wait_recv()
        for b in range(Kg):
            a = j * Kg + b
            total = u[a, mine, :]
            for p in range(1, S):
                total = total + d1[p, a].astype(F32)
            v[a] = total.astype(BF)

        @pl.when(self_lead(j))
        def _():
            d2[c, pl.ds(0, Kg)] = v[pl.ds(j * Kg, Kg)]

        @pl.when(jnp.logical_not(self_lead(j)))
        def _():
            d2_send(j).start()

    def fw_copy(src_c, dst_c):
        return remote(
            fws.at[dst_c], fwr.at[src_c], fw_ss.at[dst_c], fw_rs.at[src_c],
            (s, (dst_c * Kc) // Kr, dst_c),
        )

    def bw_copy(src_c, dst_c):
        return remote(
            xs, bwr.at[src_c], bw_ss.at[dst_c], bw_rs.at[src_c],
            (s, (dst_c * Kc) // Kr, dst_c),
        )

    def x1_copy(q, to):
        owner = lead + q
        local = c * Kc + q * Kg - owner * Kr
        return remote(
            xs.at[pl.ds(q * Kg, Kg)], x.at[pl.ds(local, Kg), mine], x1_ss.at[q, to],
            x1_rs.at[local // Kg], (s, owner, to),
        )

    def x2_copy(j, p):
        place = x.at[pl.ds(j * Kg, Kg), mine]
        return remote(place, place, x2_ss.at[j, p], x2_rs.at[j, p], (lax.rem(s + p, S), r, c))

    def x1_wait(j):
        place = x.at[pl.ds(j * Kg, Kg), mine]
        remote(place, place, x1_ss.at[0, 0], x1_rs.at[j], (s, r, c)).wait_recv()

    @pl.when(is_lead)
    def _():
        w_row(Kc - 1)
        tr_copy.wait()
        for q in range(Q):
            for o in range(C):
                def take(q=q, o=o):
                    remote(
                        v.at[pl.ds(0, Kg)], d2.at[o, pl.ds(q * Kg, Kg)], d2_ss.at[0],
                        d2_rs.at[q, o], (s, lead + q, o),
                    ).wait_recv()
                if q == 0:
                    pl.when(c != o)(take)
                else:
                    take()
        for k in range(Kc):
            total = tr[k].astype(F32)
            for o in range(C):
                total = total - d2[o, k].astype(F32)
            res[k] = total
        for o in range(C - 1):
            @pl.when(c > o)
            def _(o=o):
                fw_copy(o, c).wait_recv()
                for k in range(Kc):
                    res[k] = res[k] - fwr[o, k].astype(F32)
        rb = [res[k].astype(BF) for k in range(Kc)]
        fb = []
        for k in range(Kc):
            t = dot_nt(rb[k], W[blk(k), blk(k)])
            for b in range(k):
                t = t + dot_nt(rb[b], W[blk(k), blk(b)])
            fb.append(t.astype(BF))
            xf[k] = fb[k]
        for o in range(1, C):
            @pl.when(c < o)
            def _(o=o):
                for rr in range(R):
                    if (rr * Kr) // Kc == o:
                        tf_wait(rr)
                for k in range(Kc):
                    t = None
                    for b in range(Kc):
                        term = dot_nt(xf[b], tf[o * Kc + k, b])
                        t = term if t is None else t + term
                    fws[o, k] = t.astype(BF)
                fw_copy(c, o).start()
        for k in range(Kc):
            res[k] = xf[k].astype(F32)
        for o in range(C - 1, 0, -1):
            @pl.when(c < o)
            def _(o=o):
                bw_copy(o, c).wait_recv()
                for k in range(Kc):
                    t = res[k]
                    for a in range(Kc):
                        t = t - dot_nn(bwr[o, a], tf[o * Kc + a, k])
                    res[k] = t

                @pl.when((o * Kc) // Kr == lead)
                def _():
                    j = (o * Kc - lead * Kr) // Kg
                    x1_wait(j)
                    for p in range(1, S):
                        x2_copy(j, p).start()
        wb = [res[k].astype(BF) for k in range(Kc)]
        for k in range(Kc):
            t = dot_nn(wb[k], W[blk(k), blk(k)])
            for a in range(k + 1, Kc):
                t = t + dot_nn(wb[a], W[blk(a), blk(k)])
            xs[k] = t.astype(BF)
        for o in range(C - 2, -1, -1):
            @pl.when(c > o)
            def _(o=o):
                bw_copy(c, o).start()
        local = c * Kc - lead * Kr
        for b in range(Kg):
            x[local + b, mine, :] = xs[b]
        for p in range(1, S):
            x2_copy(local // Kg, p).start()
        for q in range(Q):
            for o in range(C):
                if q == 0:
                    @pl.when(c != o)
                    def _(q=q, o=o):
                        x1_copy(q, o).start()
                else:
                    x1_copy(q, o).start()

    def x2_from(j, p):
        src = lax.rem(s + S - p, S)
        place = x.at[pl.ds(j * Kg, Kg), pl.ds(pl.multiple_of(src * ns, ns), ns)]
        return remote(place, place, x2_ss.at[j, p], x2_rs.at[j, p], (src, r, c))

    def z_send(p):
        to = lax.rem(r + p, R)
        return remote(zb.at[p], zr.at[p], z_ss.at[p], z_rs.at[p], (s, to, c))

    for j in range(chunks - 1, -1, -1):
        @pl.when(jnp.logical_not(jnp.logical_and(is_lead, group_of(j) >= c)))
        def _():
            x1_wait(j)
            for p in range(1, S):
                x2_copy(j, p).start()
        for p in range(1, S):
            x2_from(j, p).wait_recv()
        if j == 0:
            top[...] = x[...]
        for p in [*range(1, R), 0]:
            rr = lax.rem(r + p, R)
            for i in range(Ni):
                t = None if j == chunks - 1 else acc[p, i]
                for b in range(Kg):
                    a = j * Kg + b
                    w = pat[a, rr * Ni + i].astype(F32)
                    term = dot_nn(x[a], coup[a, rr, i]) * w
                    t = term if t is None else t + term
                if j == 0 and p > 0:
                    zb[p, i] = t.astype(BF)
                else:
                    acc[p, i] = t
            if j == 0 and p > 0:
                z_send(p).start()

    for p in range(1, R):
        z_send(p).wait_recv()
    for i in range(Ni):
        t = y[r, i].astype(F32) - acc[0, i]
        for p in range(1, R):
            t = t - zr[p, i].astype(F32)
        out[i] = dot_nn(t.astype(BF), gt[i]).astype(BF)

    for p in range(1, R):
        y_send(p).wait_send()
        z_send(p).wait_send()

    @pl.when(r > lead)
    def _():
        tf_send.wait_send()

    for j in range(chunks):
        for p in range(1, S):
            d1_send(j, p).wait_send()
            x2_copy(j, p).wait_send()

        @pl.when(jnp.logical_not(self_lead(j)))
        def _():
            d2_send(j).wait_send()

    @pl.when(is_lead)
    def _():
        for o in range(C):
            @pl.when(c < o)
            def _(o=o):
                fw_copy(c, o).wait_send()

            @pl.when(c > o)
            def _(o=o):
                bw_copy(c, o).wait_send()
            for q in range(Q):
                if q == 0:
                    @pl.when(c != o)
                    def _(q=q, o=o):
                        x1_copy(q, o).wait_send()
                else:
                    x1_copy(q, o).wait_send()


def write(leaf, top, leaf_h, top_h, sem):
    copies = [
        pltpu.make_async_copy(top, top_h, sem.at[0]),
        pltpu.make_async_copy(leaf, leaf_h, sem.at[1]),
    ]
    for cp in copies:
        cp.start()
    for cp in copies:
        cp.wait()


def local(sizes, leaf_rhs, leaf_inverse, coupling, pattern, top_rhs, top_inverse, top_factor):
    S, R, C = sizes
    _, Kr, NL, _, B, _ = coupling.shape
    Ni = NL // R
    KT, n, _ = top_rhs.shape
    Kc = top_factor.shape[1]
    ns = n // S
    Kg = min(Kr, Kc)
    chunks, Q = Kr // Kg, Kc // Kg
    V = pltpu.VMEM
    D = pltpu.SemaphoreType.DMA
    any_spec = pl.BlockSpec(memory_space=pl.ANY)
    scratch = [
        V((Ni, n, B), BF), V((Ni, B, B), BF), V((Ni, B, B), BF),
        V((Kr, R, Ni, B, B), BF), V((R, Ni, n, B), BF),
        V((Kr, n, B), F32), V((Kr, n, B), BF), V((S, Kr, ns, B), BF), V((Kr, ns, B), BF),
        V((C, Kc, ns, B), BF), V((KT, Kc, B, B), BF), V((Kc, B, B), BF), V((Kc, ns, B), BF),
        V((Kc * B, Kc * B), BF), V((Kc, ns, B), F32), V((Kc, ns, B), BF),
        V((C, Kc, ns, B), BF), V((C, Kc, ns, B), BF), V((Kc, ns, B), BF), V((C, Kc, ns, B), BF),
        V((Kr, n, B), BF), V((R, Ni, n, B), F32), V((R, Ni, n, B), BF), V((R, Ni, n, B), BF),
        D((5,)), D((Kr, R)), D((R,)), D((R,)), D, D((R,)),
        D((chunks, S)), D((chunks, S)), D((chunks,)), D((Q, C)),
        D((C,)), D((C,)), D((C,)), D((C,)),
        D((Q, C)), D((chunks,)), D((chunks, S)), D((chunks, S)), D((R,)), D((R,)),
    ]
    leaf, top = pl.pallas_call(
        functools.partial(kernel, S, R, C),
        out_shape=(
            pltpu.VMEM((Ni, n, B), BF),
            pltpu.VMEM((Kr, n, B), BF),
        ),
        in_specs=[pl.BlockSpec(memory_space=pltpu.SMEM)] + [any_spec] * 6,
        out_specs=(pl.BlockSpec(memory_space=pltpu.VMEM),) * 2,
        scratch_shapes=scratch,
        compiler_params=pltpu.CompilerParams(
            collective_id=0, has_side_effects=True, vmem_limit_bytes=56 * 1024 * 1024
        ),
    )(
        pattern.reshape(Kr, NL),
        leaf_rhs.reshape(Ni, n, B),
        leaf_inverse.reshape(Ni, B, B),
        coupling.reshape(Kr, R, Ni, B, B),
        top_rhs,
        top_inverse,
        top_factor,
    )
    leaf, top = pl.pallas_call(
        write,
        out_shape=(
            jax.ShapeDtypeStruct((Ni, n, B), BF),
            jax.ShapeDtypeStruct((Kr, n, B), BF),
        ),
        in_specs=[pl.BlockSpec(memory_space=pltpu.VMEM)] * 2,
        out_specs=(any_spec, any_spec),
        scratch_shapes=[D((2,))],
        cost_estimate=pl.CostEstimate(flops=0, bytes_accessed=4 * (Ni + Kr) * n * B, transcendentals=0),
    )(leaf, top)
    return leaf[None, :, None], top


def solution(mesh):
    placed = (
        P("sub", "row", "col", None, None),
        P("sub", "row", "col", None, None),
        P("sub", "row", None, "col", None, None),
        P("sub", "row", None, "col"),
        P(),
        P(),
        P("row", "col", None, None),
    )
    sizes = tuple(mesh.shape[name] for name in ("sub", "row", "col"))
    return jax.shard_map(
        functools.partial(local, sizes),
        mesh=mesh,
        in_specs=placed,
        out_specs=(P("sub", "row", "col", None, None), P("row", None, None)),
        check_vma=False,
    )
```

```python
import functools

import jax
import jax.numpy as jnp
from jax import lax
from jax.experimental import pallas as pl
from jax.experimental.pallas import tpu as pltpu
from jax.sharding import PartitionSpec as P

BF = jnp.bfloat16
F32 = jnp.float32


def dot_nt(a, b):
    return lax.dot_general(a, b, (((1,), (1,)), ((), ())), preferred_element_type=F32)


def dot_nn(a, b):
    return lax.dot_general(a, b, (((1,), (0,)), ((), ())), preferred_element_type=F32)


def lower(block):
    rows = lax.broadcasted_iota(jnp.int32, block.shape, 0)
    cols = lax.broadcasted_iota(jnp.int32, block.shape, 1)
    return jnp.where(rows >= cols, block.astype(F32), 0.0).astype(BF)


def kernel(
    S, R, C,
    pat, rhs_h, linv_h, coup_h, trhs_h, tinv_h, tf_h,
    out, top,
    rhs, ginv, gt, coup, y, u, ub, d1, v, d2, tf, ti, tr, W, res, xf,
    fws, fwr, xs, x, acc, cx, pf, px,
    ld, cp_sem, y_ss, y_rs, tf_ss, tf_rs, d1_ss, d1_rs, d2_ss, d2_rs,
    fw_ss, fw_rs, x1_ss, x1_rs, x2_ss, x2_rs, cx_ss, cx_rs, px_ss, px_rs,
):
    s, r, c = lax.axis_index("sub"), lax.axis_index("row"), lax.axis_index("col")
    Kr, _, Ni, B, _ = coup.shape
    KT, Kc = tf.shape[:2]
    n = y.shape[2]
    ns = n // S
    Kg = min(Kr, Kc)
    chunks = Kr // Kg
    Q = Kc // Kg
    lead = (c * Kc) // Kr
    is_lead = r == lead
    mine = pl.ds(pl.multiple_of(s * ns, ns), ns)

    def remote(src, dst, ss, rs, dev):
        return pltpu.make_async_remote_copy(
            src_ref=src, dst_ref=dst, send_sem=ss, recv_sem=rs,
            device_id=dev, device_id_type=pl.DeviceIdType.MESH,
        )

    def group_of(j):
        return (r * Kr + j * Kg) // Kc

    loads = [
        pltpu.make_async_copy(linv_h, ginv, ld.at[0]),
        pltpu.make_async_copy(rhs_h, rhs, ld.at[1]),
    ]
    for cp in loads:
        cp.start()

    def coup_copy(a, p):
        rr = lax.rem(r + p, R)
        return pltpu.make_async_copy(coup_h.at[a, rr], coup.at[a, rr], cp_sem.at[a, p])

    for j in range(chunks):
        for p in range(R):
            for a in range(j * Kg, (j + 1) * Kg):
                coup_copy(a, p).start()
    ti_copy = pltpu.make_async_copy(tinv_h.at[pl.ds(c * Kc, Kc)], ti, ld.at[2])
    tr_copy = pltpu.make_async_copy(trhs_h.at[pl.ds(c * Kc, Kc), mine], tr, ld.at[3])
    tf_copy = pltpu.make_async_copy(tf_h, tf.at[pl.ds(r * Kr, Kr)], ld.at[4])

    @pl.when(is_lead)
    def _():
        ti_copy.start()
        tr_copy.start()
        tf_copy.start()

    barrier = pltpu.get_barrier_semaphore()
    for p in range(1, S):
        pl.semaphore_signal(
            barrier, inc=1, device_id=(lax.rem(s + p, S), r, c), device_id_type=pl.DeviceIdType.MESH
        )
    for p in range(R):
        for q in range(C):
            if p == 0 and q == 0:
                continue
            pl.semaphore_signal(
                barrier, inc=1, device_id=(s, lax.rem(r + p, R), lax.rem(c + q, C)),
                device_id_type=pl.DeviceIdType.MESH,
            )

    for cp in loads:
        cp.wait()
    for i in range(Ni):
        g = lower(ginv[i])
        gt[i] = g
        y[r, i] = dot_nt(rhs[i], g).astype(BF)

    pl.semaphore_wait(barrier, S - 1 + R * C - 1)

    def y_send(p):
        return remote(y.at[r], y.at[r], y_ss.at[p], y_rs.at[p], (s, lax.rem(r + p, R), c))

    def y_from(p):
        src = lax.rem(r + R - p, R)
        return remote(y.at[src], y.at[src], y_ss.at[p], y_rs.at[p], (s, src, c))

    for p in range(1, R):
        y_send(p).start()

    tf_send = remote(tf_h, tf.at[pl.ds(r * Kr, Kr)], tf_ss, tf_rs.at[r], (s, lead, c))

    @pl.when(r > lead)
    def _():
        tf_send.start()

    def tf_wait(rr):
        remote(tf_h, tf.at[pl.ds(rr * Kr, Kr)], tf_ss, tf_rs.at[rr], (s, lead, c)).wait_recv()

    def add(a, rr, first):
        total = None if first else u[a]
        for i in range(Ni):
            w = pat[a, rr * Ni + i].astype(F32)
            term = dot_nt(y[rr, i], coup[a, rr, i]) * w
            total = term if total is None else total + term
        return total

    def d1_send(j, p):
        to = lax.rem(s + p, S)
        rows = pl.ds(pl.multiple_of(to * ns, ns), ns)
        blocks = pl.ds(j * Kg, Kg)
        return remote(
            ub.at[blocks, rows], d1.at[p, blocks], d1_ss.at[j, p], d1_rs.at[j, p], (to, r, c)
        )

    for j in range(chunks):
        blocks = range(j * Kg, (j + 1) * Kg)
        for p in range(R):
            if j == 0 and p > 0:
                y_from(R - p).wait_recv()
            for a in blocks:
                coup_copy(a, p).wait()
            for a in blocks:
                total = add(a, lax.rem(r + p, R), p == 0)
                u[a] = total
                if p == R - 1:
                    ub[a] = total.astype(BF)
        for t in range(1, S):
            d1_send(j, t).start()

    def d2_send(j):
        g = group_of(j)
        pos = lax.rem(r * Kr + j * Kg, Kc)
        return remote(
            v.at[pl.ds(j * Kg, Kg)], d2.at[c, pl.ds(pos, Kg)], d2_ss.at[j],
            d2_rs.at[pos // Kg, c], (s, (g * Kc) // Kr, g),
        )

    def self_lead(j):
        return jnp.logical_and(is_lead, group_of(j) == c)

    def blk(k):
        return pl.ds(k * B, B)

    def w_row(k):
        g = lower(ti[k])
        W[blk(k), blk(k)] = g
        for b in range(k):
            t = None
            for m in range(b, k):
                term = dot_nn(tf[c * Kc + k, m], W[blk(m), blk(b)])
                t = term if t is None else t + term
            W[blk(k), blk(b)] = (-dot_nn(g, t.astype(BF))).astype(BF)

    for j in range(chunks):
        for p in range(1, S):
            d1_send(j, p).wait_recv()
        for b in range(Kg):
            a = j * Kg + b
            total = u[a, mine, :]
            for p in range(1, S):
                total = total + d1[p, a].astype(F32)
            v[a] = total.astype(BF)

        @pl.when(self_lead(j))
        def _():
            d2[c, pl.ds(0, Kg)] = v[pl.ds(j * Kg, Kg)]

        @pl.when(jnp.logical_not(self_lead(j)))
        def _():
            d2_send(j).start()

    def cx_send(p):
        to = lax.rem(r + p, R)
        return remote(coup_h.at[:, to], cx.at[r], cx_ss.at[p], cx_rs.at[r], (s, to, c))

    def px_send(p):
        to = lax.rem(r + p, R)
        return remote(pf.at[to], px.at[r], px_ss.at[p], px_rs.at[r], (s, to, c))

    cx_own = pltpu.make_async_copy(coup_h.at[:, r], cx.at[r], ld.at[5])
    cx_own.start()
    for p in range(1, R):
        cx_send(p).start()
    for rr in range(R):
        for a in range(Kr):
            for i in range(Ni):
                pf[rr, a, i] = jnp.full((8, B), pat[a, rr * Ni + i].astype(F32))
    px[r] = pf[r]
    for p in range(1, R):
        px_send(p).start()

    def fw_copy(src_c, dst_c):
        return remote(
            fws.at[dst_c], fwr.at[src_c], fw_ss.at[dst_c], fw_rs.at[src_c],
            (s, (dst_c * Kc) // Kr, dst_c),
        )

    def x1_copy(rr, o):
        return remote(
            xs, x.at[pl.ds(c * Kc, Kc), mine], x1_ss.at[rr, o], x1_rs.at[c], (s, rr, o)
        )

    def lead_of(o):
        return (o * Kc) // Kr

    def x2_copy(g, p):
        place = x.at[pl.ds(g * Kc, Kc), mine]
        return remote(place, place, x2_ss.at[g, p], x2_rs.at[g, p], (lax.rem(s + p, S), r, c))

    def x1_wait(g):
        place = x.at[pl.ds(g * Kc, Kc), mine]
        remote(place, place, x1_ss.at[0, 0], x1_rs.at[g], (s, r, c)).wait_recv()

    @pl.when(is_lead)
    def _():
        ti_copy.wait()
        tf_copy.wait()
        for q in range(1, Q):
            tf_wait(lead + q)
        for k in range(Kc):
            w_row(k)
        tr_copy.wait()
        for q in range(Q):
            for o in range(C):
                def take(q=q, o=o):
                    remote(
                        v.at[pl.ds(0, Kg)], d2.at[o, pl.ds(q * Kg, Kg)], d2_ss.at[0],
                        d2_rs.at[q, o], (s, lead + q, o),
                    ).wait_recv()
                if q == 0:
                    pl.when(c != o)(take)
                else:
                    take()
        for k in range(Kc):
            total = tr[k].astype(F32)
            for o in range(C):
                total = total - d2[o, k].astype(F32)
            res[k] = total
        for o in range(C - 1):
            @pl.when(c > o)
            def _(o=o):
                fw_copy(o, c).wait_recv()
                for k in range(Kc):
                    res[k] = res[k] - fwr[o, k].astype(F32)
        rb = [res[k].astype(BF) for k in range(Kc)]
        fb = []
        for k in range(Kc):
            t = dot_nt(rb[k], W[blk(k), blk(k)])
            for b in range(k):
                t = t + dot_nt(rb[b], W[blk(k), blk(b)])
            fb.append(t.astype(BF))
            xf[k] = fb[k]
        for o in range(1, C):
            @pl.when(c < o)
            def _(o=o):
                for rr in range(R):
                    if (rr * Kr) // Kc == o:
                        tf_wait(rr)
                for k in range(Kc):
                    t = None
                    for b in range(Kc):
                        term = dot_nt(xf[b], tf[o * Kc + k, b])
                        t = term if t is None else t + term
                    fws[o, k] = t.astype(BF)
                fw_copy(c, o).start()
        for k in range(Kc):
            res[k] = xf[k].astype(F32)
        for o in range(C - 1, 0, -1):
            @pl.when(c < o)
            def _(o=o):
                x1_wait(o)
                for k in range(Kc):
                    t = res[k]
                    for a in range(Kc):
                        t = t - dot_nn(x[o * Kc + a, mine, :], tf[o * Kc + a, k])
                    res[k] = t
                for p in range(1, S):
                    x2_copy(o, p).start()
        wb = [res[k].astype(BF) for k in range(Kc)]
        for k in range(Kc):
            t = dot_nn(wb[k], W[blk(k), blk(k)])
            for a in range(k + 1, Kc):
                t = t + dot_nn(wb[a], W[blk(a), blk(k)])
            xs[k] = t.astype(BF)
        for o in range(C - 2, -1, -1):
            @pl.when(c > o)
            def _(o=o):
                x1_copy(lead_of(o), o).start()
        for b in range(Kc):
            x[c * Kc + b, mine, :] = xs[b]
        for p in range(1, S):
            x2_copy(c, p).start()
        for rr in range(R):
            for o in range(C):
                if rr != lead_of(o):
                    x1_copy(rr, o).start()
                else:
                    @pl.when(c < o)
                    def _(rr=rr, o=o):
                        x1_copy(rr, o).start()

    def x2_from(g, p):
        src = lax.rem(s + S - p, S)
        place = x.at[pl.ds(g * Kc, Kc), pl.ds(pl.multiple_of(src * ns, ns), ns)]
        return remote(place, place, x2_ss.at[g, p], x2_rs.at[g, p], (src, r, c))

    cx_own.wait()
    for p in range(1, R):
        src = lax.rem(r + p, R)
        remote(coup_h.at[:, r], cx.at[src], cx_ss.at[p], cx_rs.at[src], (s, src, c)).wait_recv()
        remote(pf.at[r], px.at[src], px_ss.at[p], px_rs.at[src], (s, src, c)).wait_recv()

    for g in range(C - 1, -1, -1):
        @pl.when(jnp.logical_not(jnp.logical_and(is_lead, c <= g)))
        def _():
            x1_wait(g)
            for p in range(1, S):
                x2_copy(g, p).start()
        for p in range(1, S):
            x2_from(g, p).wait_recv()
        for i in range(Ni):
            t = y[r, i].astype(F32) if g == C - 1 else acc[i]
            for b in range(Kc):
                a = g * Kc + b
                owner, at = a // Kr, a % Kr
                t = t - dot_nn(x[a], cx[owner, at, i]) * px[owner, at, i, 0:1, :]
            if g > 0:
                acc[i] = t
            else:
                out[i] = dot_nn(t.astype(BF), gt[i]).astype(BF)
    top[...] = x[pl.ds(r * Kr, Kr)]

    for p in range(1, R):
        y_send(p).wait_send()
        cx_send(p).wait_send()
        px_send(p).wait_send()

    @pl.when(r > lead)
    def _():
        tf_send.wait_send()

    for j in range(chunks):
        for p in range(1, S):
            d1_send(j, p).wait_send()

        @pl.when(jnp.logical_not(self_lead(j)))
        def _():
            d2_send(j).wait_send()

    for g in range(C):
        for p in range(1, S):
            x2_copy(g, p).wait_send()

    @pl.when(is_lead)
    def _():
        for o in range(C):
            @pl.when(c < o)
            def _(o=o):
                fw_copy(c, o).wait_send()

            for rr in range(R):
                if rr != lead_of(o):
                    x1_copy(rr, o).wait_send()
                else:
                    @pl.when(c != o)
                    def _(rr=rr, o=o):
                        x1_copy(rr, o).wait_send()


def local(sizes, leaf_rhs, leaf_inverse, coupling, pattern, top_rhs, top_inverse, top_factor):
    S, R, C = sizes
    _, Kr, NL, _, B, _ = coupling.shape
    Ni = NL // R
    KT, n, _ = top_rhs.shape
    Kc = top_factor.shape[1]
    ns = n // S
    Kg = min(Kr, Kc)
    chunks, Q = Kr // Kg, Kc // Kg
    V = pltpu.VMEM
    D = pltpu.SemaphoreType.DMA
    any_spec = pl.BlockSpec(memory_space=pl.ANY)
    scratch = [
        V((Ni, n, B), BF), V((Ni, B, B), BF), V((Ni, B, B), BF),
        V((Kr, R, Ni, B, B), BF), V((R, Ni, n, B), BF),
        V((Kr, n, B), F32), V((Kr, n, B), BF), V((S, Kr, ns, B), BF), V((Kr, ns, B), BF),
        V((C, Kc, ns, B), BF), V((KT, Kc, B, B), BF), V((Kc, B, B), BF), V((Kc, ns, B), BF),
        V((Kc * B, Kc * B), BF), V((Kc, ns, B), F32), V((Kc, ns, B), BF),
        V((C, Kc, ns, B), BF), V((C, Kc, ns, B), BF), V((Kc, ns, B), BF),
        V((KT, n, B), BF), V((Ni, n, B), F32), V((R, Kr, Ni, B, B), BF),
        V((R, Kr, Ni, 8, B), F32), V((R, Kr, Ni, 8, B), F32),
        D((6,)), D((Kr, R)), D((R,)), D((R,)), D, D((R,)),
        D((chunks, S)), D((chunks, S)), D((chunks,)), D((Q, C)),
        D((C,)), D((C,)),
        D((R, C)), D((C,)), D((C, S)), D((C, S)), D((R,)), D((R,)), D((R,)), D((R,)),
    ]
    leaf, top = pl.pallas_call(
        functools.partial(kernel, S, R, C),
        out_shape=(
            pltpu.VMEM((Ni, n, B), BF),
            pltpu.VMEM((Kr, n, B), BF),
        ),
        in_specs=[pl.BlockSpec(memory_space=pltpu.SMEM)] + [any_spec] * 6,
        out_specs=(pl.BlockSpec(memory_space=pltpu.VMEM),) * 2,
        scratch_shapes=scratch,
        compiler_params=pltpu.CompilerParams(
            collective_id=0, has_side_effects=True, vmem_limit_bytes=56 * 1024 * 1024
        ),
    )(
        pattern.reshape(Kr, NL),
        leaf_rhs.reshape(Ni, n, B),
        leaf_inverse.reshape(Ni, B, B),
        coupling.reshape(Kr, R, Ni, B, B),
        top_rhs,
        top_inverse,
        top_factor,
    )
    return leaf[None, :, None], top


def solution(mesh):
    placed = (
        P("sub", "row", "col", None, None),
        P("sub", "row", "col", None, None),
        P("sub", "row", None, "col", None, None),
        P("sub", "row", None, "col"),
        P(),
        P(),
        P("row", "col", None, None),
    )
    sizes = tuple(mesh.shape[name] for name in ("sub", "row", "col"))
    return jax.shard_map(
        functools.partial(local, sizes),
        mesh=mesh,
        in_specs=placed,
        out_specs=(P("sub", "row", "col", None, None), P("row", None, None)),
        check_vma=False,
    )
```

```python
import functools

import jax
import jax.numpy as jnp
from jax import lax
from jax.experimental import pallas as pl
from jax.experimental.pallas import tpu as pltpu
from jax.sharding import PartitionSpec as P

BF = jnp.bfloat16
F32 = jnp.float32


def dot_nt(a, b):
    return lax.dot_general(a, b, (((1,), (1,)), ((), ())), preferred_element_type=F32)


def dot_nn(a, b):
    return lax.dot_general(a, b, (((1,), (0,)), ((), ())), preferred_element_type=F32)


def lower(block):
    rows = lax.broadcasted_iota(jnp.int32, block.shape, 0)
    cols = lax.broadcasted_iota(jnp.int32, block.shape, 1)
    return jnp.where(rows >= cols, block.astype(F32), 0.0).astype(BF)


def kernel(
    S, R, C,
    pat, rhs_h, linv_h, coup_h, trhs_h, tinv_h, tf_h,
    out, top,
    rhs, ginv, gt, coup, y, u, ub, d1, v, d2, tf, ti, tr, W, FW, res, xf,
    fws, fwr, xs, x, acc, cx, pf, px,
    ld, cp_sem, y_ss, y_rs, tf_ss, tf_rs, d1_ss, d1_rs, d2_ss, d2_rs,
    fw_ss, fw_rs, x1_ss, x1_rs, x2_ss, x2_rs, cx_ss, cx_rs, px_ss, px_rs,
):
    s, r, c = lax.axis_index("sub"), lax.axis_index("row"), lax.axis_index("col")
    Kr, _, Ni, B, _ = coup.shape
    KT, Kc = tf.shape[:2]
    n = y.shape[2]
    ns = n // S
    Kg = min(Kr, Kc)
    chunks = Kr // Kg
    Q = Kc // Kg
    lead = (c * Kc) // Kr
    is_lead = r == lead
    mine = pl.ds(pl.multiple_of(s * ns, ns), ns)

    def remote(src, dst, ss, rs, dev):
        return pltpu.make_async_remote_copy(
            src_ref=src, dst_ref=dst, send_sem=ss, recv_sem=rs,
            device_id=dev, device_id_type=pl.DeviceIdType.MESH,
        )

    def group_of(j):
        return (r * Kr + j * Kg) // Kc

    loads = [
        pltpu.make_async_copy(linv_h, ginv, ld.at[0]),
        pltpu.make_async_copy(rhs_h, rhs, ld.at[1]),
    ]
    for cp in loads:
        cp.start()

    def coup_copy(a, p):
        rr = lax.rem(r + p, R)
        return pltpu.make_async_copy(coup_h.at[a, rr], coup.at[a, rr], cp_sem.at[a, p])

    for j in range(chunks):
        for p in range(R):
            for a in range(j * Kg, (j + 1) * Kg):
                coup_copy(a, p).start()
    ti_copy = pltpu.make_async_copy(tinv_h.at[pl.ds(c * Kc, Kc)], ti, ld.at[2])
    tr_copy = pltpu.make_async_copy(trhs_h.at[pl.ds(c * Kc, Kc), mine], tr, ld.at[3])
    tf_copy = pltpu.make_async_copy(tf_h, tf.at[pl.ds(r * Kr, Kr)], ld.at[4])

    @pl.when(is_lead)
    def _():
        ti_copy.start()
        tr_copy.start()
        tf_copy.start()

    barrier = pltpu.get_barrier_semaphore()
    for p in range(1, S):
        pl.semaphore_signal(
            barrier, inc=1, device_id=(lax.rem(s + p, S), r, c), device_id_type=pl.DeviceIdType.MESH
        )
    for p in range(R):
        for q in range(C):
            if p == 0 and q == 0:
                continue
            pl.semaphore_signal(
                barrier, inc=1, device_id=(s, lax.rem(r + p, R), lax.rem(c + q, C)),
                device_id_type=pl.DeviceIdType.MESH,
            )

    for cp in loads:
        cp.wait()
    for i in range(Ni):
        g = lower(ginv[i])
        gt[i] = g
        y[r, i] = dot_nt(rhs[i], g).astype(BF)

    pl.semaphore_wait(barrier, S - 1 + R * C - 1)

    def y_send(p):
        return remote(y.at[r], y.at[r], y_ss.at[p], y_rs.at[p], (s, lax.rem(r + p, R), c))

    def y_from(p):
        src = lax.rem(r + R - p, R)
        return remote(y.at[src], y.at[src], y_ss.at[p], y_rs.at[p], (s, src, c))

    for p in range(1, R):
        y_send(p).start()

    tf_send = remote(tf_h, tf.at[pl.ds(r * Kr, Kr)], tf_ss, tf_rs.at[r], (s, lead, c))

    @pl.when(r > lead)
    def _():
        tf_send.start()

    def tf_wait(rr):
        remote(tf_h, tf.at[pl.ds(rr * Kr, Kr)], tf_ss, tf_rs.at[rr], (s, lead, c)).wait_recv()

    def add(a, rr, first):
        total = None if first else u[a]
        for i in range(Ni):
            w = pat[a, rr * Ni + i].astype(F32)
            term = dot_nt(y[rr, i], coup[a, rr, i]) * w
            total = term if total is None else total + term
        return total

    def d1_send(j, p):
        to = lax.rem(s + p, S)
        rows = pl.ds(pl.multiple_of(to * ns, ns), ns)
        blocks = pl.ds(j * Kg, Kg)
        return remote(
            ub.at[blocks, rows], d1.at[p, blocks], d1_ss.at[j, p], d1_rs.at[j, p], (to, r, c)
        )

    for j in range(chunks):
        blocks = range(j * Kg, (j + 1) * Kg)
        for p in range(R):
            if j == 0 and p > 0:
                y_from(R - p).wait_recv()
            for a in blocks:
                coup_copy(a, p).wait()
            for a in blocks:
                total = add(a, lax.rem(r + p, R), p == 0)
                u[a] = total
                if p == R - 1:
                    ub[a] = total.astype(BF)
        for t in range(1, S):
            d1_send(j, t).start()

    def d2_send(j):
        g = group_of(j)
        pos = lax.rem(r * Kr + j * Kg, Kc)
        return remote(
            v.at[pl.ds(j * Kg, Kg)], d2.at[c, pl.ds(pos, Kg)], d2_ss.at[j],
            d2_rs.at[pos // Kg, c], (s, (g * Kc) // Kr, g),
        )

    def self_lead(j):
        return jnp.logical_and(is_lead, group_of(j) == c)

    def blk(k):
        return pl.ds(k * B, B)

    def w_row(k):
        g = lower(ti[k])
        W[blk(k), blk(k)] = g
        for b in range(k):
            t = None
            for m in range(b, k):
                term = dot_nn(tf[c * Kc + k, m], W[blk(m), blk(b)])
                t = term if t is None else t + term
            W[blk(k), blk(b)] = (-dot_nn(g, t.astype(BF))).astype(BF)

    for j in range(chunks):
        for p in range(1, S):
            d1_send(j, p).wait_recv()
        for b in range(Kg):
            a = j * Kg + b
            total = u[a, mine, :]
            for p in range(1, S):
                total = total + d1[p, a].astype(F32)
            v[a] = total.astype(BF)

        @pl.when(self_lead(j))
        def _():
            d2[c, pl.ds(0, Kg)] = v[pl.ds(j * Kg, Kg)]

        @pl.when(jnp.logical_not(self_lead(j)))
        def _():
            d2_send(j).start()

    def cx_send(p):
        to = lax.rem(r + p, R)
        return remote(coup_h.at[:, to], cx.at[r], cx_ss.at[p], cx_rs.at[r], (s, to, c))

    def px_send(p):
        to = lax.rem(r + p, R)
        return remote(pf.at[to], px.at[r], px_ss.at[p], px_rs.at[r], (s, to, c))

    cx_own = pltpu.make_async_copy(coup_h.at[:, r], cx.at[r], ld.at[5])
    cx_own.start()
    for p in range(1, R):
        cx_send(p).start()
    for rr in range(R):
        for a in range(Kr):
            for i in range(Ni):
                pf[rr, a, i] = jnp.full((8, B), pat[a, rr * Ni + i].astype(F32))
    px[r] = pf[r]
    for p in range(1, R):
        px_send(p).start()

    def fw_copy(src_c, dst_c):
        return remote(
            fws.at[dst_c], fwr.at[src_c], fw_ss.at[dst_c], fw_rs.at[src_c],
            (s, (dst_c * Kc) // Kr, dst_c),
        )

    def x1_copy(rr, o):
        return remote(
            xs, x.at[pl.ds(c * Kc, Kc), mine], x1_ss.at[rr, o], x1_rs.at[c], (s, rr, o)
        )

    def lead_of(o):
        return (o * Kc) // Kr

    def x2_copy(g, p, rr):
        place = x.at[pl.ds(g * Kc, Kc), mine]
        return remote(
            place, place, x2_ss.at[g, rr, p], x2_rs.at[g, p], (lax.rem(s + p, S), rr, c)
        )

    def x2_each(g, act):
        @pl.when(r == lead_of(g))
        def _():
            for rr in range(R):
                for p in range(S):
                    if p > 0:
                        act(x2_copy(g, p, rr))
                    else:
                        has = jnp.logical_or(rr == r, jnp.logical_and(rr == lead, c < g))

                        @pl.when(jnp.logical_not(has))
                        def _(rr=rr):
                            act(x2_copy(g, 0, rr))

    def x2_forward(g):
        x2_each(g, lambda copy: copy.start())

    def x1_wait(g):
        place = x.at[pl.ds(g * Kc, Kc), mine]
        remote(place, place, x1_ss.at[0, 0], x1_rs.at[g], (s, r, c)).wait_recv()

    @pl.when(is_lead)
    def _():
        ti_copy.wait()
        tf_copy.wait()
        for q in range(1, Q):
            tf_wait(lead + q)
        for k in range(Kc):
            w_row(k)

        def next_products():
            def row(k, carry):
                for b in range(Kc):
                    t = None
                    for m in range(b, Kc):
                        term = dot_nn(tf[(c + 1) * Kc + k, m], W[blk(m), blk(b)])
                        t = term if t is None else t + term
                    FW[pl.ds(pl.multiple_of(k * B, B), B), blk(b)] = t.astype(BF)
                return carry

            lax.fori_loop(0, Kc, row, 0)

        @pl.when(c > 0)
        def _():
            for rr in range(R):
                @pl.when(rr >= lead + Q)
                def _(rr=rr):
                    tf_wait(rr)

        @pl.when(jnp.logical_and(c > 0, c < C - 1))
        def _():
            next_products()

        tr_copy.wait()
        for q in range(Q):
            for o in range(C):
                def take(q=q, o=o):
                    remote(
                        v.at[pl.ds(0, Kg)], d2.at[o, pl.ds(q * Kg, Kg)], d2_ss.at[0],
                        d2_rs.at[q, o], (s, lead + q, o),
                    ).wait_recv()
                if q == 0:
                    pl.when(c != o)(take)
                else:
                    take()
        for k in range(Kc):
            total = tr[k].astype(F32)
            for o in range(C):
                total = total - d2[o, k].astype(F32)
            res[k] = total
        for o in range(C - 1):
            @pl.when(c > o)
            def _(o=o):
                fw_copy(o, c).wait_recv()
                for k in range(Kc):
                    res[k] = res[k] - fwr[o, k].astype(F32)
        rb = [res[k].astype(BF) for k in range(Kc)]

        @pl.when(jnp.logical_and(c > 0, c < C - 1))
        def _():
            for k in range(Kc):
                t = None
                for b in range(Kc):
                    term = dot_nt(rb[b], FW[blk(k), blk(b)])
                    t = term if t is None else t + term
                fws[c + 1, k] = t.astype(BF)
            fw_copy(c, c + 1).start()

        for k in range(Kc):
            t = dot_nt(rb[k], W[blk(k), blk(k)])
            for b in range(k):
                t = t + dot_nt(rb[b], W[blk(k), blk(b)])
            xf[k] = t.astype(BF)

        def give(o):
            for k in range(Kc):
                t = None
                for b in range(Kc):
                    term = dot_nt(xf[b], tf[o * Kc + k, b])
                    t = term if t is None else t + term
                fws[o, k] = t.astype(BF)
            fw_copy(c, o).start()

        @pl.when(c == 0)
        def _():
            for rr in range(R):
                if (rr * Kr) // Kc == 1:
                    tf_wait(rr)
            give(1)
            for rr in range(R):
                if (rr * Kr) // Kc > 1:
                    tf_wait(rr)

        for o in range(2, C):
            @pl.when(c < o - 1)
            def _(o=o):
                give(o)

        @pl.when(c == 0)
        def _():
            next_products()
        for k in range(Kc):
            res[k] = xf[k].astype(F32)
        for o in range(C - 1, 1, -1):
            @pl.when(c < o - 1)
            def _(o=o):
                x1_wait(o)
                for k in range(Kc):
                    t = res[k]
                    for a in range(Kc):
                        t = t - dot_nn(x[o * Kc + a, mine, :], tf[o * Kc + a, k])
                    res[k] = t
                x2_forward(o)
        wb = [res[k].astype(BF) for k in range(Kc)]
        for k in range(Kc):
            t = dot_nn(wb[k], W[blk(k), blk(k)])
            for a in range(k + 1, Kc):
                t = t + dot_nn(wb[a], W[blk(a), blk(k)])
            res[k] = t

        @pl.when(c < C - 1)
        def _():
            x1_wait(c + 1)
            for k in range(Kc):
                t = res[k]
                for a in range(Kc):
                    t = t - dot_nn(x[(c + 1) * Kc + a, mine, :], FW[blk(a), blk(k)])
                res[k] = t
        for k in range(Kc):
            xs[k] = res[k].astype(BF)
        for o in range(C - 2, -1, -1):
            @pl.when(c > o)
            def _(o=o):
                x1_copy(lead_of(o), o).start()
        for o in range(C - 1, -1, -1):
            @pl.when(jnp.logical_and(c != o, jnp.logical_or(c < o, lead_of(o) != lead)))
            def _(o=o):
                x1_copy(lead, o).start()
        for b in range(Kc):
            x[c * Kc + b, mine, :] = xs[b]
        x2_forward(c)

        @pl.when(c < C - 1)
        def _():
            x2_forward(c + 1)

    def x2_from(g, p):
        src = lax.rem(s + S - p, S)
        row = lead_of(g)
        place = x.at[pl.ds(g * Kc, Kc), pl.ds(pl.multiple_of(src * ns, ns), ns)]
        return remote(place, place, x2_ss.at[g, row, p], x2_rs.at[g, p], (src, row, c))

    cx_own.wait()
    for p in range(1, R):
        src = lax.rem(r + p, R)
        remote(coup_h.at[:, r], cx.at[src], cx_ss.at[p], cx_rs.at[src], (s, src, c)).wait_recv()
        remote(pf.at[r], px.at[src], px_ss.at[p], px_rs.at[src], (s, src, c)).wait_recv()

    for g in range(C - 1, -1, -1):
        late = jnp.logical_not(jnp.logical_and(is_lead, c <= g))

        @pl.when(jnp.logical_and(late, r == lead_of(g)))
        def _():
            x1_wait(g)
            x2_forward(g)

        @pl.when(jnp.logical_and(late, r != lead_of(g)))
        def _():
            x2_from(g, 0).wait_recv()

        for p in range(1, S):
            x2_from(g, p).wait_recv()
        for i in range(Ni):
            t = y[r, i].astype(F32) if g == C - 1 else acc[i]
            for b in range(Kc):
                a = g * Kc + b
                owner, at = a // Kr, a % Kr
                t = t - dot_nn(x[a], cx[owner, at, i]) * px[owner, at, i, 0:1, :]
            if g > 0:
                acc[i] = t
            else:
                out[i] = dot_nn(t.astype(BF), gt[i]).astype(BF)
    top[...] = x[pl.ds(r * Kr, Kr)]

    for p in range(1, R):
        y_send(p).wait_send()
        cx_send(p).wait_send()
        px_send(p).wait_send()

    @pl.when(r > lead)
    def _():
        tf_send.wait_send()

    for j in range(chunks):
        for p in range(1, S):
            d1_send(j, p).wait_send()

        @pl.when(jnp.logical_not(self_lead(j)))
        def _():
            d2_send(j).wait_send()

    for g in range(C):
        x2_each(g, lambda copy: copy.wait_send())

    @pl.when(is_lead)
    def _():
        for o in range(C):
            @pl.when(c < o)
            def _(o=o):
                fw_copy(c, o).wait_send()

            @pl.when(jnp.logical_and(c != o, c > o))
            def _(o=o):
                x1_copy(lead_of(o), o).wait_send()

            @pl.when(jnp.logical_and(c != o, jnp.logical_or(c < o, lead_of(o) != lead)))
            def _(o=o):
                x1_copy(lead, o).wait_send()


def local(sizes, leaf_rhs, leaf_inverse, coupling, pattern, top_rhs, top_inverse, top_factor):
    S, R, C = sizes
    _, Kr, NL, _, B, _ = coupling.shape
    Ni = NL // R
    KT, n, _ = top_rhs.shape
    Kc = top_factor.shape[1]
    ns = n // S
    Kg = min(Kr, Kc)
    chunks, Q = Kr // Kg, Kc // Kg
    V = pltpu.VMEM
    D = pltpu.SemaphoreType.DMA
    any_spec = pl.BlockSpec(memory_space=pl.ANY)
    scratch = [
        V((Ni, n, B), BF), V((Ni, B, B), BF), V((Ni, B, B), BF),
        V((Kr, R, Ni, B, B), BF), V((R, Ni, n, B), BF),
        V((Kr, n, B), F32), V((Kr, n, B), BF), V((S, Kr, ns, B), BF), V((Kr, ns, B), BF),
        V((C, Kc, ns, B), BF), V((KT, Kc, B, B), BF), V((Kc, B, B), BF), V((Kc, ns, B), BF),
        V((Kc * B, Kc * B), BF), V((Kc * B, Kc * B), BF), V((Kc, ns, B), F32), V((Kc, ns, B), BF),
        V((C, Kc, ns, B), BF), V((C, Kc, ns, B), BF), V((Kc, ns, B), BF),
        V((KT, n, B), BF), V((Ni, n, B), F32), V((R, Kr, Ni, B, B), BF),
        V((R, Kr, Ni, 8, B), F32), V((R, Kr, Ni, 8, B), F32),
        D((6,)), D((Kr, R)), D((R,)), D((R,)), D, D((R,)),
        D((chunks, S)), D((chunks, S)), D((chunks,)), D((Q, C)),
        D((C,)), D((C,)),
        D((R, C)), D((C,)), D((C, R, S)), D((C, S)), D((R,)), D((R,)), D((R,)), D((R,)),
    ]
    leaf, top = pl.pallas_call(
        functools.partial(kernel, S, R, C),
        out_shape=(
            pltpu.VMEM((Ni, n, B), BF),
            pltpu.VMEM((Kr, n, B), BF),
        ),
        in_specs=[pl.BlockSpec(memory_space=pltpu.SMEM)] + [any_spec] * 6,
        out_specs=(pl.BlockSpec(memory_space=pltpu.VMEM),) * 2,
        scratch_shapes=scratch,
        compiler_params=pltpu.CompilerParams(
            collective_id=0, has_side_effects=True, vmem_limit_bytes=56 * 1024 * 1024
        ),
    )(
        pattern.reshape(Kr, NL),
        leaf_rhs.reshape(Ni, n, B),
        leaf_inverse.reshape(Ni, B, B),
        coupling.reshape(Kr, R, Ni, B, B),
        top_rhs,
        top_inverse,
        top_factor,
    )
    return leaf[None, :, None], top


def solution(mesh):
    placed = (
        P("sub", "row", "col", None, None),
        P("sub", "row", "col", None, None),
        P("sub", "row", None, "col", None, None),
        P("sub", "row", None, "col"),
        P(),
        P(),
        P("row", "col", None, None),
    )
    sizes = tuple(mesh.shape[name] for name in ("sub", "row", "col"))
    return jax.shard_map(
        functools.partial(local, sizes),
        mesh=mesh,
        in_specs=placed,
        out_specs=(P("sub", "row", "col", None, None), P("row", None, None)),
        check_vma=False,
    )
```

```python
import functools

import jax
import jax.numpy as jnp
from jax import lax
from jax.experimental import pallas as pl
from jax.experimental.pallas import tpu as pltpu
from jax.sharding import PartitionSpec as P

BF = jnp.bfloat16
F32 = jnp.float32


def dot_nt(a, b):
    return lax.dot_general(a, b, (((1,), (1,)), ((), ())), preferred_element_type=F32)


def dot_nn(a, b):
    return lax.dot_general(a, b, (((1,), (0,)), ((), ())), preferred_element_type=F32)


def lower(block):
    rows = lax.broadcasted_iota(jnp.int32, block.shape, 0)
    cols = lax.broadcasted_iota(jnp.int32, block.shape, 1)
    return jnp.where(rows >= cols, block.astype(F32), 0.0).astype(BF)


def kernel(
    S, R, C,
    pat, rhs_h, linv_h, coup_h, trhs_h, tinv_h, tf_h,
    out, top,
    rhs, ginv, gt, coup, y, u, ub, d1, v, d2, tf, ti, tr, W, FW, res, xf,
    fws, fwr, xs, x, acc, cx, pf, px,
    ld, cp_sem, y_ss, y_rs, tf_ss, tf_rs, d1_ss, d1_rs, d2_ss, d2_rs,
    fw_ss, fw_rs, x1_ss, x1_rs, x2_ss, x2_rs, cx_ss, cx_rs, px_ss, px_rs,
):
    s, r, c = lax.axis_index("sub"), lax.axis_index("row"), lax.axis_index("col")
    Kr, _, Ni, B, _ = coup.shape
    KT, Kc = tf.shape[:2]
    n = y.shape[2]
    ns = n // S
    Kg = min(Kr, Kc)
    chunks = Kr // Kg
    Q = Kc // Kg
    lead = (c * Kc) // Kr
    is_lead = r == lead
    mine = pl.ds(pl.multiple_of(s * ns, ns), ns)

    def remote(src, dst, ss, rs, dev):
        return pltpu.make_async_remote_copy(
            src_ref=src, dst_ref=dst, send_sem=ss, recv_sem=rs,
            device_id=dev, device_id_type=pl.DeviceIdType.MESH,
        )

    def group_of(j):
        return (r * Kr + j * Kg) // Kc

    loads = [
        pltpu.make_async_copy(linv_h, ginv, ld.at[0]),
        pltpu.make_async_copy(rhs_h, rhs, ld.at[1]),
    ]
    for cp in loads:
        cp.start()

    def coup_copy(a, p):
        rr = lax.rem(r + p, R)
        return pltpu.make_async_copy(coup_h.at[a, rr], coup.at[a, rr], cp_sem.at[a, p])

    ti_copy = pltpu.make_async_copy(tinv_h.at[pl.ds(c * Kc, Kc)], ti, ld.at[2])
    tr_copy = pltpu.make_async_copy(trhs_h.at[pl.ds(c * Kc, Kc), mine], tr, ld.at[3])
    tf_copy = pltpu.make_async_copy(tf_h, tf.at[pl.ds(r * Kr, Kr)], ld.at[4])

    barrier = pltpu.get_barrier_semaphore()
    for p in range(1, S):
        pl.semaphore_signal(
            barrier, inc=1, device_id=(lax.rem(s + p, S), r, c), device_id_type=pl.DeviceIdType.MESH
        )
    for p in range(R):
        for q in range(C):
            if p == 0 and q == 0:
                continue
            pl.semaphore_signal(
                barrier, inc=1, device_id=(s, lax.rem(r + p, R), lax.rem(c + q, C)),
                device_id_type=pl.DeviceIdType.MESH,
            )

    for rr in range(R):
        for a in range(Kr):
            for i in range(Ni):
                pf[rr, a, i] = jnp.full((8, B), pat[a, rr * Ni + i].astype(F32))
    px[r] = pf[r]
    for cp in loads:
        cp.wait()
    for j in range(chunks):
        for p in range(R):
            for a in range(j * Kg, (j + 1) * Kg):
                coup_copy(a, p).start()

    @pl.when(is_lead)
    def _():
        ti_copy.start()
        tr_copy.start()
        tf_copy.start()

    for i in range(Ni):
        g = lower(ginv[i])
        gt[i] = g
        y[r, i] = dot_nt(rhs[i], g).astype(BF)

    pl.semaphore_wait(barrier, S - 1 + R * C - 1)

    def y_send(p):
        return remote(y.at[r], y.at[r], y_ss.at[p], y_rs.at[p], (s, lax.rem(r + p, R), c))

    def y_from(p):
        src = lax.rem(r + R - p, R)
        return remote(y.at[src], y.at[src], y_ss.at[p], y_rs.at[p], (s, src, c))

    for p in range(1, R):
        y_send(p).start()

    tf_send = remote(tf_h, tf.at[pl.ds(r * Kr, Kr)], tf_ss, tf_rs.at[r], (s, lead, c))

    @pl.when(r > lead)
    def _():
        tf_send.start()

    def tf_wait(rr):
        remote(tf_h, tf.at[pl.ds(rr * Kr, Kr)], tf_ss, tf_rs.at[rr], (s, lead, c)).wait_recv()

    def add(a, rr, first):
        total = None if first else u[a]
        for i in range(Ni):
            w = pat[a, rr * Ni + i].astype(F32)
            term = dot_nt(y[rr, i], coup[a, rr, i]) * w
            total = term if total is None else total + term
        return total

    def d1_send(j, p):
        to = lax.rem(s + p, S)
        rows = pl.ds(pl.multiple_of(to * ns, ns), ns)
        blocks = pl.ds(j * Kg, Kg)
        return remote(
            ub.at[blocks, rows], d1.at[p, blocks], d1_ss.at[j, p], d1_rs.at[j, p], (to, r, c)
        )

    for j in range(chunks):
        blocks = range(j * Kg, (j + 1) * Kg)
        for p in range(R):
            if j == 0 and p > 0:
                y_from(R - p).wait_recv()
            for a in blocks:
                coup_copy(a, p).wait()
            for a in blocks:
                total = add(a, lax.rem(r + p, R), p == 0)
                u[a] = total
                if p == R - 1:
                    ub[a] = total.astype(BF)
        for t in range(1, S):
            d1_send(j, t).start()

    def d2_send(j):
        g = group_of(j)
        pos = lax.rem(r * Kr + j * Kg, Kc)
        return remote(
            v.at[pl.ds(j * Kg, Kg)], d2.at[c, pl.ds(pos, Kg)], d2_ss.at[j],
            d2_rs.at[pos // Kg, c], (s, (g * Kc) // Kr, g),
        )

    def self_lead(j):
        return jnp.logical_and(is_lead, group_of(j) == c)

    def cx_send(p):
        to = lax.rem(r + p, R)
        return remote(coup_h.at[:, to], cx.at[r], cx_ss.at[p], cx_rs.at[r], (s, to, c))

    def px_send(p):
        to = lax.rem(r + p, R)
        return remote(pf.at[to], px.at[r], px_ss.at[p], px_rs.at[r], (s, to, c))

    cx_own = pltpu.make_async_copy(coup_h.at[:, r], cx.at[r], ld.at[5])
    cx_own.start()
    for p in range(1, R):
        cx_send(p).start()
    for p in range(1, R):
        px_send(p).start()

    def blk(k):
        return pl.ds(k * B, B)

    def w_row(k):
        g = lower(ti[k])
        W[blk(k), blk(k)] = g
        for b in range(k):
            t = None
            for m in range(b, k):
                term = dot_nn(tf[c * Kc + k, m], W[blk(m), blk(b)])
                t = term if t is None else t + term
            W[blk(k), blk(b)] = (-dot_nn(g, t.astype(BF))).astype(BF)

    def group_inverse():
        ti_copy.wait()
        tf_copy.wait()
        for q in range(1, Q):
            tf_wait(lead + q)
        for k in range(Kc):
            w_row(k)

    @pl.when(jnp.logical_and(is_lead, c == 0))
    def _():
        group_inverse()

    for j in range(chunks):
        for p in range(1, S):
            d1_send(j, p).wait_recv()
        for b in range(Kg):
            a = j * Kg + b
            total = u[a, mine, :]
            for p in range(1, S):
                total = total + d1[p, a].astype(F32)
            v[a] = total.astype(BF)

        @pl.when(self_lead(j))
        def _():
            d2[c, pl.ds(0, Kg)] = v[pl.ds(j * Kg, Kg)]

        @pl.when(jnp.logical_not(self_lead(j)))
        def _():
            d2_send(j).start()

    def fw_copy(src_c, dst_c):
        return remote(
            fws.at[dst_c], fwr.at[src_c], fw_ss.at[dst_c], fw_rs.at[src_c],
            (s, (dst_c * Kc) // Kr, dst_c),
        )

    def x1_copy(rr, o):
        return remote(
            xs, x.at[pl.ds(c * Kc, Kc), mine], x1_ss.at[rr, o], x1_rs.at[c], (s, rr, o)
        )

    def lead_of(o):
        return (o * Kc) // Kr

    def x2_copy(g, p, rr):
        place = x.at[pl.ds(g * Kc, Kc), mine]
        return remote(
            place, place, x2_ss.at[g, rr, p], x2_rs.at[g, p], (lax.rem(s + p, S), rr, c)
        )

    def x2_each(g, act):
        @pl.when(r == lead_of(g))
        def _():
            for rr in range(R):
                for p in range(S):
                    if p > 0:
                        act(x2_copy(g, p, rr))
                    else:
                        has = jnp.logical_or(rr == r, jnp.logical_and(rr == lead, c < g))

                        @pl.when(jnp.logical_not(has))
                        def _(rr=rr):
                            act(x2_copy(g, 0, rr))

    def x2_forward(g):
        x2_each(g, lambda copy: copy.start())

    def x1_wait(g):
        place = x.at[pl.ds(g * Kc, Kc), mine]
        remote(place, place, x1_ss.at[0, 0], x1_rs.at[g], (s, r, c)).wait_recv()

    @pl.when(is_lead)
    def _():
        @pl.when(c > 0)
        def _():
            group_inverse()

        def next_products():
            def row(k, carry):
                for b in range(Kc):
                    t = None
                    for m in range(b, Kc):
                        term = dot_nn(tf[(c + 1) * Kc + k, m], W[blk(m), blk(b)])
                        t = term if t is None else t + term
                    FW[pl.ds(pl.multiple_of(k * B, B), B), blk(b)] = t.astype(BF)
                return carry

            lax.fori_loop(0, Kc, row, 0)

        @pl.when(c > 0)
        def _():
            for rr in range(R):
                @pl.when(rr >= lead + Q)
                def _(rr=rr):
                    tf_wait(rr)

        @pl.when(jnp.logical_and(c > 0, c < C - 1))
        def _():
            next_products()

        tr_copy.wait()
        for q in range(Q):
            for o in range(C):
                def take(q=q, o=o):
                    remote(
                        v.at[pl.ds(0, Kg)], d2.at[o, pl.ds(q * Kg, Kg)], d2_ss.at[0],
                        d2_rs.at[q, o], (s, lead + q, o),
                    ).wait_recv()
                if q == 0:
                    pl.when(c != o)(take)
                else:
                    take()
        for k in range(Kc):
            total = tr[k].astype(F32)
            for o in range(C):
                total = total - d2[o, k].astype(F32)
            res[k] = total
        for o in range(C - 1):
            @pl.when(c > o)
            def _(o=o):
                fw_copy(o, c).wait_recv()
                for k in range(Kc):
                    res[k] = res[k] - fwr[o, k].astype(F32)
        rb = [res[k].astype(BF) for k in range(Kc)]

        @pl.when(jnp.logical_and(c > 0, c < C - 1))
        def _():
            for k in range(Kc):
                t = None
                for b in range(Kc):
                    term = dot_nt(rb[b], FW[blk(k), blk(b)])
                    t = term if t is None else t + term
                fws[c + 1, k] = t.astype(BF)
            fw_copy(c, c + 1).start()

        for k in range(Kc):
            t = dot_nt(rb[k], W[blk(k), blk(k)])
            for b in range(k):
                t = t + dot_nt(rb[b], W[blk(k), blk(b)])
            xf[k] = t.astype(BF)

        def give(o):
            for k in range(Kc):
                t = None
                for b in range(Kc):
                    term = dot_nt(xf[b], tf[o * Kc + k, b])
                    t = term if t is None else t + term
                fws[o, k] = t.astype(BF)
            fw_copy(c, o).start()

        @pl.when(c == 0)
        def _():
            for rr in range(R):
                if (rr * Kr) // Kc == 1:
                    tf_wait(rr)
            give(1)
            for rr in range(R):
                if (rr * Kr) // Kc > 1:
                    tf_wait(rr)

        for o in range(2, C):
            @pl.when(c < o - 1)
            def _(o=o):
                give(o)

        @pl.when(c == 0)
        def _():
            next_products()
        for k in range(Kc):
            res[k] = xf[k].astype(F32)
        for o in range(C - 1, 1, -1):
            @pl.when(c < o - 1)
            def _(o=o):
                x1_wait(o)
                for k in range(Kc):
                    t = res[k]
                    for a in range(Kc):
                        t = t - dot_nn(x[o * Kc + a, mine, :], tf[o * Kc + a, k])
                    res[k] = t
                x2_forward(o)
        wb = [res[k].astype(BF) for k in range(Kc)]
        for k in range(Kc):
            t = dot_nn(wb[k], W[blk(k), blk(k)])
            for a in range(k + 1, Kc):
                t = t + dot_nn(wb[a], W[blk(a), blk(k)])
            res[k] = t

        @pl.when(c < C - 1)
        def _():
            x1_wait(c + 1)
            for k in range(Kc):
                t = res[k]
                for a in range(Kc):
                    t = t - dot_nn(x[(c + 1) * Kc + a, mine, :], FW[blk(a), blk(k)])
                res[k] = t
        for k in range(Kc):
            xs[k] = res[k].astype(BF)
        for o in range(C - 2, -1, -1):
            @pl.when(c > o)
            def _(o=o):
                x1_copy(lead_of(o), o).start()
        for o in range(C - 1, -1, -1):
            @pl.when(jnp.logical_and(c != o, jnp.logical_or(c < o, lead_of(o) != lead)))
            def _(o=o):
                x1_copy(lead, o).start()
        for b in range(Kc):
            x[c * Kc + b, mine, :] = xs[b]
        x2_forward(c)

        @pl.when(c < C - 1)
        def _():
            x2_forward(c + 1)

    def x2_from(g, p):
        src = lax.rem(s + S - p, S)
        row = lead_of(g)
        place = x.at[pl.ds(g * Kc, Kc), pl.ds(pl.multiple_of(src * ns, ns), ns)]
        return remote(place, place, x2_ss.at[g, row, p], x2_rs.at[g, p], (src, row, c))

    cx_own.wait()
    for p in range(1, R):
        src = lax.rem(r + p, R)
        remote(coup_h.at[:, r], cx.at[src], cx_ss.at[p], cx_rs.at[src], (s, src, c)).wait_recv()
        remote(pf.at[r], px.at[src], px_ss.at[p], px_rs.at[src], (s, src, c)).wait_recv()

    for g in range(C - 1, -1, -1):
        late = jnp.logical_not(jnp.logical_and(is_lead, c <= g))

        @pl.when(jnp.logical_and(late, r == lead_of(g)))
        def _():
            x1_wait(g)
            x2_forward(g)

        @pl.when(jnp.logical_and(late, r != lead_of(g)))
        def _():
            x2_from(g, 0).wait_recv()

        for p in range(1, S):
            x2_from(g, p).wait_recv()
        for i in range(Ni):
            t = y[r, i].astype(F32) if g == C - 1 else acc[i]
            for b in range(Kc):
                a = g * Kc + b
                owner, at = a // Kr, a % Kr
                t = t - dot_nn(x[a], cx[owner, at, i]) * px[owner, at, i, 0:1, :]
            if g > 0:
                acc[i] = t
            else:
                out[i] = dot_nn(t.astype(BF), gt[i]).astype(BF)
    top[...] = x[pl.ds(r * Kr, Kr)]

    for p in range(1, R):
        y_send(p).wait_send()
        cx_send(p).wait_send()
        px_send(p).wait_send()

    @pl.when(r > lead)
    def _():
        tf_send.wait_send()

    for j in range(chunks):
        for p in range(1, S):
            d1_send(j, p).wait_send()

        @pl.when(jnp.logical_not(self_lead(j)))
        def _():
            d2_send(j).wait_send()

    for g in range(C):
        x2_each(g, lambda copy: copy.wait_send())

    @pl.when(is_lead)
    def _():
        for o in range(C):
            @pl.when(c < o)
            def _(o=o):
                fw_copy(c, o).wait_send()

            @pl.when(jnp.logical_and(c != o, c > o))
            def _(o=o):
                x1_copy(lead_of(o), o).wait_send()

            @pl.when(jnp.logical_and(c != o, jnp.logical_or(c < o, lead_of(o) != lead)))
            def _(o=o):
                x1_copy(lead, o).wait_send()


def local(sizes, leaf_rhs, leaf_inverse, coupling, pattern, top_rhs, top_inverse, top_factor):
    S, R, C = sizes
    _, Kr, NL, _, B, _ = coupling.shape
    Ni = NL // R
    KT, n, _ = top_rhs.shape
    Kc = top_factor.shape[1]
    ns = n // S
    Kg = min(Kr, Kc)
    chunks, Q = Kr // Kg, Kc // Kg
    V = pltpu.VMEM
    D = pltpu.SemaphoreType.DMA
    any_spec = pl.BlockSpec(memory_space=pl.ANY)
    scratch = [
        V((Ni, n, B), BF), V((Ni, B, B), BF), V((Ni, B, B), BF),
        V((Kr, R, Ni, B, B), BF), V((R, Ni, n, B), BF),
        V((Kr, n, B), F32), V((Kr, n, B), BF), V((S, Kr, ns, B), BF), V((Kr, ns, B), BF),
        V((C, Kc, ns, B), BF), V((KT, Kc, B, B), BF), V((Kc, B, B), BF), V((Kc, ns, B), BF),
        V((Kc * B, Kc * B), BF), V((Kc * B, Kc * B), BF), V((Kc, ns, B), F32), V((Kc, ns, B), BF),
        V((C, Kc, ns, B), BF), V((C, Kc, ns, B), BF), V((Kc, ns, B), BF),
        V((KT, n, B), BF), V((Ni, n, B), F32), V((R, Kr, Ni, B, B), BF),
        V((R, Kr, Ni, 8, B), F32), V((R, Kr, Ni, 8, B), F32),
        D((6,)), D((Kr, R)), D((R,)), D((R,)), D, D((R,)),
        D((chunks, S)), D((chunks, S)), D((chunks,)), D((Q, C)),
        D((C,)), D((C,)),
        D((R, C)), D((C,)), D((C, R, S)), D((C, S)), D((R,)), D((R,)), D((R,)), D((R,)),
    ]
    leaf, top = pl.pallas_call(
        functools.partial(kernel, S, R, C),
        out_shape=(
            pltpu.VMEM((Ni, n, B), BF),
            pltpu.VMEM((Kr, n, B), BF),
        ),
        in_specs=[pl.BlockSpec(memory_space=pltpu.SMEM)] + [any_spec] * 6,
        out_specs=(pl.BlockSpec(memory_space=pltpu.VMEM),) * 2,
        scratch_shapes=scratch,
        compiler_params=pltpu.CompilerParams(
            collective_id=0, has_side_effects=True, vmem_limit_bytes=56 * 1024 * 1024
        ),
    )(
        pattern.reshape(Kr, NL),
        leaf_rhs.reshape(Ni, n, B),
        leaf_inverse.reshape(Ni, B, B),
        coupling.reshape(Kr, R, Ni, B, B),
        top_rhs,
        top_inverse,
        top_factor,
    )
    return leaf[None, :, None], top


def solution(mesh):
    placed = (
        P("sub", "row", "col", None, None),
        P("sub", "row", "col", None, None),
        P("sub", "row", None, "col", None, None),
        P("sub", "row", None, "col"),
        P(),
        P(),
        P("row", "col", None, None),
    )
    sizes = tuple(mesh.shape[name] for name in ("sub", "row", "col"))
    return jax.shard_map(
        functools.partial(local, sizes),
        mesh=mesh,
        in_specs=placed,
        out_specs=(P("sub", "row", "col", None, None), P("row", None, None)),
        check_vma=False,
    )
```

```python
import functools

import jax
import jax.numpy as jnp
from jax import lax
from jax.experimental import pallas as pl
from jax.experimental.pallas import tpu as pltpu
from jax.sharding import PartitionSpec as P

BF = jnp.bfloat16
F32 = jnp.float32


def dot_nt(a, b):
    return lax.dot_general(a, b, (((1,), (1,)), ((), ())), preferred_element_type=F32)


def dot_nn(a, b):
    return lax.dot_general(a, b, (((1,), (0,)), ((), ())), preferred_element_type=F32)


def lower(block):
    rows = lax.broadcasted_iota(jnp.int32, block.shape, 0)
    cols = lax.broadcasted_iota(jnp.int32, block.shape, 1)
    return jnp.where(rows >= cols, block.astype(F32), 0.0).astype(BF)


def kernel(
    S, R, C,
    pat, rhs_h, linv_h, coup_h, trhs_h, tinv_h, tf_h,
    out, top,
    rhs, ginv, gt, coup, y, u, ub, d1, v, d2, tf, ti, tr, W, FW, res, xf,
    fws, fwr, xs, x, acc, cx, pf, px,
    ld, cp_sem, y_ss, y_rs, tf_ss, tf_rs, d1_ss, d1_rs, d2_ss, d2_rs,
    fw_ss, fw_rs, x1_ss, x1_rs, x2_ss, x2_rs, cx_ss, cx_rs, px_ss, px_rs,
):
    s, r, c = lax.axis_index("sub"), lax.axis_index("row"), lax.axis_index("col")
    Kr, _, Ni, B, _ = coup.shape
    KT, Kc = tf.shape[:2]
    n = y.shape[2]
    ns = n // S
    Kg = min(Kr, Kc)
    chunks = Kr // Kg
    Q = Kc // Kg
    lead = (c * Kc) // Kr
    is_lead = r == lead
    mine = pl.ds(pl.multiple_of(s * ns, ns), ns)

    def remote(src, dst, ss, rs, dev):
        return pltpu.make_async_remote_copy(
            src_ref=src, dst_ref=dst, send_sem=ss, recv_sem=rs,
            device_id=dev, device_id_type=pl.DeviceIdType.MESH,
        )

    def group_of(j):
        return (r * Kr + j * Kg) // Kc

    loads = [
        pltpu.make_async_copy(linv_h, ginv, ld.at[0]),
        pltpu.make_async_copy(rhs_h, rhs, ld.at[1]),
    ]
    for cp in loads:
        cp.start()

    def coup_copy(a, p):
        rr = lax.rem(r + p, R)
        return pltpu.make_async_copy(coup_h.at[a, rr], coup.at[a, rr], cp_sem.at[a, p])

    ti_copy = pltpu.make_async_copy(tinv_h.at[pl.ds(c * Kc, Kc)], ti, ld.at[2])
    tr_copy = pltpu.make_async_copy(trhs_h.at[pl.ds(c * Kc, Kc), mine], tr, ld.at[3])
    tf_copy = pltpu.make_async_copy(tf_h, tf.at[pl.ds(r * Kr, Kr)], ld.at[4])

    barrier = pltpu.get_barrier_semaphore()
    for p in range(1, S):
        pl.semaphore_signal(
            barrier, inc=1, device_id=(lax.rem(s + p, S), r, c), device_id_type=pl.DeviceIdType.MESH
        )
    for p in range(R):
        for q in range(C):
            if p == 0 and q == 0:
                continue
            pl.semaphore_signal(
                barrier, inc=1, device_id=(s, lax.rem(r + p, R), lax.rem(c + q, C)),
                device_id_type=pl.DeviceIdType.MESH,
            )

    for rr in range(R):
        for a in range(Kr):
            for i in range(Ni):
                pf[rr, a, i] = jnp.full((8, B), pat[a, rr * Ni + i].astype(F32))
    px[r] = pf[r]
    for cp in loads:
        cp.wait()
    for j in range(chunks):
        for p in range(R):
            for a in range(j * Kg, (j + 1) * Kg):
                coup_copy(a, p).start()

    @pl.when(is_lead)
    def _():
        ti_copy.start()
        tr_copy.start()
        tf_copy.start()

    for i in range(Ni):
        g = lower(ginv[i])
        gt[i] = g
        y[r, i] = dot_nt(rhs[i], g).astype(BF)

    pl.semaphore_wait(barrier, S - 1 + R * C - 1)

    def y_send(p):
        return remote(y.at[r], y.at[r], y_ss.at[p], y_rs.at[p], (s, lax.rem(r + p, R), c))

    def y_from(p):
        src = lax.rem(r + R - p, R)
        return remote(y.at[src], y.at[src], y_ss.at[p], y_rs.at[p], (s, src, c))

    for p in range(1, R):
        y_send(p).start()

    tf_send = remote(tf_h, tf.at[pl.ds(r * Kr, Kr)], tf_ss, tf_rs.at[r], (s, lead, c))

    @pl.when(r > lead)
    def _():
        tf_send.start()

    def tf_wait(rr):
        remote(tf_h, tf.at[pl.ds(rr * Kr, Kr)], tf_ss, tf_rs.at[rr], (s, lead, c)).wait_recv()

    def add(a, rr, first):
        total = None if first else u[a]
        for i in range(Ni):
            w = pat[a, rr * Ni + i].astype(F32)
            term = dot_nt(y[rr, i], coup[a, rr, i]) * w
            total = term if total is None else total + term
        return total

    def d1_send(j, p):
        to = lax.rem(s + p, S)
        rows = pl.ds(pl.multiple_of(to * ns, ns), ns)
        blocks = pl.ds(j * Kg, Kg)
        return remote(
            ub.at[blocks, rows], d1.at[p, blocks], d1_ss.at[j, p], d1_rs.at[j, p], (to, r, c)
        )

    for j in range(chunks):
        blocks = range(j * Kg, (j + 1) * Kg)
        for p in range(R):
            if j == 0 and p > 0:
                y_from(R - p).wait_recv()
            for a in blocks:
                coup_copy(a, p).wait()
            for a in blocks:
                total = add(a, lax.rem(r + p, R), p == 0)
                u[a] = total
                if p == R - 1:
                    ub[a] = total.astype(BF)
        for t in range(1, S):
            d1_send(j, t).start()

    def d2_send(j):
        g = group_of(j)
        pos = lax.rem(r * Kr + j * Kg, Kc)
        return remote(
            v.at[pl.ds(j * Kg, Kg)], d2.at[c, pl.ds(pos, Kg)], d2_ss.at[j],
            d2_rs.at[pos // Kg, c], (s, (g * Kc) // Kr, g),
        )

    def self_lead(j):
        return jnp.logical_and(is_lead, group_of(j) == c)

    def blk(k):
        return pl.ds(k * B, B)

    def w_row(k):
        g = lower(ti[k])
        W[blk(k), blk(k)] = g
        for b in range(k):
            t = None
            for m in range(b, k):
                term = dot_nn(tf[c * Kc + k, m], W[blk(m), blk(b)])
                t = term if t is None else t + term
            W[blk(k), blk(b)] = (-dot_nn(g, t.astype(BF))).astype(BF)

    def group_inverse():
        ti_copy.wait()
        tf_copy.wait()
        for q in range(1, Q):
            tf_wait(lead + q)
        for k in range(Kc):
            w_row(k)

    @pl.when(jnp.logical_and(is_lead, c == 0))
    def _():
        group_inverse()

    for j in range(chunks):
        for p in range(1, S):
            d1_send(j, p).wait_recv()
        for b in range(Kg):
            a = j * Kg + b
            total = u[a, mine, :]
            for p in range(1, S):
                total = total + d1[p, a].astype(F32)
            v[a] = total.astype(BF)

        @pl.when(self_lead(j))
        def _():
            d2[c, pl.ds(0, Kg)] = v[pl.ds(j * Kg, Kg)]

        @pl.when(jnp.logical_not(self_lead(j)))
        def _():
            d2_send(j).start()

    def cx_send(p):
        to = lax.rem(r + p, R)
        return remote(coup_h.at[:, to], cx.at[r], cx_ss.at[p], cx_rs.at[r], (s, to, c))

    def px_send(p):
        to = lax.rem(r + p, R)
        return remote(pf.at[to], px.at[r], px_ss.at[p], px_rs.at[r], (s, to, c))

    cx_own = pltpu.make_async_copy(coup_h.at[:, r], cx.at[r], ld.at[5])
    cx_own.start()
    for p in range(1, R):
        cx_send(p).start()
    for p in range(1, R):
        px_send(p).start()

    def fw_copy(src_c, dst_c):
        return remote(
            fws.at[dst_c], fwr.at[src_c], fw_ss.at[dst_c], fw_rs.at[src_c],
            (s, (dst_c * Kc) // Kr, dst_c),
        )

    def x1_copy(rr, o):
        return remote(
            xs, x.at[pl.ds(c * Kc, Kc), mine], x1_ss.at[rr, o], x1_rs.at[c], (s, rr, o)
        )

    def lead_of(o):
        return (o * Kc) // Kr

    def x2_copy(g, p, rr):
        place = x.at[pl.ds(g * Kc, Kc), mine]
        return remote(
            place, place, x2_ss.at[g, rr, p], x2_rs.at[g, p], (lax.rem(s + p, S), rr, c)
        )

    def x2_each(g, act):
        @pl.when(r == lead_of(g))
        def _():
            for rr in range(R):
                for p in range(S):
                    if p > 0:
                        act(x2_copy(g, p, rr))
                    else:
                        has = jnp.logical_or(rr == r, jnp.logical_and(rr == lead, c < g))

                        @pl.when(jnp.logical_not(has))
                        def _(rr=rr):
                            act(x2_copy(g, 0, rr))

    def x2_forward(g):
        x2_each(g, lambda copy: copy.start())

    def x1_wait(g):
        place = x.at[pl.ds(g * Kc, Kc), mine]
        remote(place, place, x1_ss.at[0, 0], x1_rs.at[g], (s, r, c)).wait_recv()

    @pl.when(is_lead)
    def _():
        @pl.when(c > 0)
        def _():
            group_inverse()

        def next_products():
            def row(k, carry):
                for b in range(Kc):
                    t = None
                    for m in range(b, Kc):
                        term = dot_nn(tf[(c + 1) * Kc + k, m], W[blk(m), blk(b)])
                        t = term if t is None else t + term
                    FW[pl.ds(pl.multiple_of(k * B, B), B), blk(b)] = t.astype(BF)
                return carry

            lax.fori_loop(0, Kc, row, 0)

        @pl.when(c > 1)
        def _():
            for rr in range(R):
                @pl.when(rr >= lead + Q)
                def _(rr=rr):
                    tf_wait(rr)

        @pl.when(jnp.logical_and(c > 1, c < C - 1))
        def _():
            next_products()

        tr_copy.wait()
        for q in range(Q):
            for o in range(C):
                def take(q=q, o=o):
                    remote(
                        v.at[pl.ds(0, Kg)], d2.at[o, pl.ds(q * Kg, Kg)], d2_ss.at[0],
                        d2_rs.at[q, o], (s, lead + q, o),
                    ).wait_recv()
                if q == 0:
                    pl.when(c != o)(take)
                else:
                    take()
        for k in range(Kc):
            total = tr[k].astype(F32)
            for o in range(C):
                total = total - d2[o, k].astype(F32)
            res[k] = total
        for o in range(C - 1):
            @pl.when(c > o)
            def _(o=o):
                fw_copy(o, c).wait_recv()
                for k in range(Kc):
                    res[k] = res[k] - fwr[o, k].astype(F32)
        rb = [res[k].astype(BF) for k in range(Kc)]

        @pl.when(jnp.logical_and(c > 1, c < C - 1))
        def _():
            for k in range(Kc):
                t = None
                for b in range(Kc):
                    term = dot_nt(rb[b], FW[blk(k), blk(b)])
                    t = term if t is None else t + term
                fws[c + 1, k] = t.astype(BF)
            fw_copy(c, c + 1).start()

        for k in range(Kc):
            t = dot_nt(rb[k], W[blk(k), blk(k)])
            for b in range(k):
                t = t + dot_nt(rb[b], W[blk(k), blk(b)])
            xf[k] = t.astype(BF)

        def give(o):
            for k in range(Kc):
                t = None
                for b in range(Kc):
                    term = dot_nt(xf[b], tf[o * Kc + k, b])
                    t = term if t is None else t + term
                fws[o, k] = t.astype(BF)
            fw_copy(c, o).start()

        for first in range(2):
            @pl.when(c == first)
            def _(first=first):
                for rr in range(R):
                    if (rr * Kr) // Kc == first + 1:
                        tf_wait(rr)
                give(first + 1)
                for rr in range(R):
                    if (rr * Kr) // Kc > first + 1:
                        tf_wait(rr)

        for o in range(2, C):
            @pl.when(c < o - 1)
            def _(o=o):
                give(o)

        @pl.when(c <= 1)
        def _():
            next_products()
        for k in range(Kc):
            res[k] = xf[k].astype(F32)
        for o in range(C - 1, 1, -1):
            @pl.when(c < o - 1)
            def _(o=o):
                x1_wait(o)
                for k in range(Kc):
                    t = res[k]
                    for a in range(Kc):
                        t = t - dot_nn(x[o * Kc + a, mine, :], tf[o * Kc + a, k])
                    res[k] = t
                x2_forward(o)
        wb = [res[k].astype(BF) for k in range(Kc)]
        for k in range(Kc):
            t = dot_nn(wb[k], W[blk(k), blk(k)])
            for a in range(k + 1, Kc):
                t = t + dot_nn(wb[a], W[blk(a), blk(k)])
            res[k] = t

        @pl.when(c < C - 1)
        def _():
            x1_wait(c + 1)
            for k in range(Kc):
                t = res[k]
                for a in range(Kc):
                    t = t - dot_nn(x[(c + 1) * Kc + a, mine, :], FW[blk(a), blk(k)])
                res[k] = t
        for k in range(Kc):
            xs[k] = res[k].astype(BF)
        for o in range(C - 2, -1, -1):
            @pl.when(c > o)
            def _(o=o):
                x1_copy(lead_of(o), o).start()
        for o in range(C - 1, -1, -1):
            @pl.when(jnp.logical_and(c != o, jnp.logical_or(c < o, lead_of(o) != lead)))
            def _(o=o):
                x1_copy(lead, o).start()
        for b in range(Kc):
            x[c * Kc + b, mine, :] = xs[b]
        x2_forward(c)

        @pl.when(c < C - 1)
        def _():
            x2_forward(c + 1)

    def x2_from(g, p):
        src = lax.rem(s + S - p, S)
        row = lead_of(g)
        place = x.at[pl.ds(g * Kc, Kc), pl.ds(pl.multiple_of(src * ns, ns), ns)]
        return remote(place, place, x2_ss.at[g, row, p], x2_rs.at[g, p], (src, row, c))

    cx_own.wait()
    for p in range(1, R):
        src = lax.rem(r + p, R)
        remote(coup_h.at[:, r], cx.at[src], cx_ss.at[p], cx_rs.at[src], (s, src, c)).wait_recv()
        remote(pf.at[r], px.at[src], px_ss.at[p], px_rs.at[src], (s, src, c)).wait_recv()

    for g in range(C - 1, -1, -1):
        late = jnp.logical_not(jnp.logical_and(is_lead, c <= g))

        @pl.when(jnp.logical_and(late, r == lead_of(g)))
        def _():
            x1_wait(g)
            x2_forward(g)

        @pl.when(jnp.logical_and(late, r != lead_of(g)))
        def _():
            x2_from(g, 0).wait_recv()

        for p in range(1, S):
            x2_from(g, p).wait_recv()
        for i in range(Ni):
            t = y[r, i].astype(F32) if g == C - 1 else acc[i]
            for b in range(Kc):
                a = g * Kc + b
                owner, at = a // Kr, a % Kr
                t = t - dot_nn(x[a], cx[owner, at, i]) * px[owner, at, i, 0:1, :]
            if g > 0:
                acc[i] = t
            else:
                out[i] = dot_nn(t.astype(BF), gt[i]).astype(BF)
    top[...] = x[pl.ds(r * Kr, Kr)]

    for p in range(1, R):
        y_send(p).wait_send()
        cx_send(p).wait_send()
        px_send(p).wait_send()

    @pl.when(r > lead)
    def _():
        tf_send.wait_send()

    for j in range(chunks):
        for p in range(1, S):
            d1_send(j, p).wait_send()

        @pl.when(jnp.logical_not(self_lead(j)))
        def _():
            d2_send(j).wait_send()

    for g in range(C):
        x2_each(g, lambda copy: copy.wait_send())

    @pl.when(is_lead)
    def _():
        for o in range(C):
            @pl.when(c < o)
            def _(o=o):
                fw_copy(c, o).wait_send()

            @pl.when(jnp.logical_and(c != o, c > o))
            def _(o=o):
                x1_copy(lead_of(o), o).wait_send()

            @pl.when(jnp.logical_and(c != o, jnp.logical_or(c < o, lead_of(o) != lead)))
            def _(o=o):
                x1_copy(lead, o).wait_send()


def local(sizes, leaf_rhs, leaf_inverse, coupling, pattern, top_rhs, top_inverse, top_factor):
    S, R, C = sizes
    _, Kr, NL, _, B, _ = coupling.shape
    Ni = NL // R
    KT, n, _ = top_rhs.shape
    Kc = top_factor.shape[1]
    ns = n // S
    Kg = min(Kr, Kc)
    chunks, Q = Kr // Kg, Kc // Kg
    V = pltpu.VMEM
    D = pltpu.SemaphoreType.DMA
    any_spec = pl.BlockSpec(memory_space=pl.ANY)
    scratch = [
        V((Ni, n, B), BF), V((Ni, B, B), BF), V((Ni, B, B), BF),
        V((Kr, R, Ni, B, B), BF), V((R, Ni, n, B), BF),
        V((Kr, n, B), F32), V((Kr, n, B), BF), V((S, Kr, ns, B), BF), V((Kr, ns, B), BF),
        V((C, Kc, ns, B), BF), V((KT, Kc, B, B), BF), V((Kc, B, B), BF), V((Kc, ns, B), BF),
        V((Kc * B, Kc * B), BF), V((Kc * B, Kc * B), BF), V((Kc, ns, B), F32), V((Kc, ns, B), BF),
        V((C, Kc, ns, B), BF), V((C, Kc, ns, B), BF), V((Kc, ns, B), BF),
        V((KT, n, B), BF), V((Ni, n, B), F32), V((R, Kr, Ni, B, B), BF),
        V((R, Kr, Ni, 8, B), F32), V((R, Kr, Ni, 8, B), F32),
        D((6,)), D((Kr, R)), D((R,)), D((R,)), D, D((R,)),
        D((chunks, S)), D((chunks, S)), D((chunks,)), D((Q, C)),
        D((C,)), D((C,)),
        D((R, C)), D((C,)), D((C, R, S)), D((C, S)), D((R,)), D((R,)), D((R,)), D((R,)),
    ]
    leaf, top = pl.pallas_call(
        functools.partial(kernel, S, R, C),
        out_shape=(
            pltpu.VMEM((Ni, n, B), BF),
            pltpu.VMEM((Kr, n, B), BF),
        ),
        in_specs=[pl.BlockSpec(memory_space=pltpu.SMEM)] + [any_spec] * 6,
        out_specs=(pl.BlockSpec(memory_space=pltpu.VMEM),) * 2,
        scratch_shapes=scratch,
        compiler_params=pltpu.CompilerParams(
            collective_id=0, has_side_effects=True, vmem_limit_bytes=56 * 1024 * 1024
        ),
    )(
        pattern.reshape(Kr, NL),
        leaf_rhs.reshape(Ni, n, B),
        leaf_inverse.reshape(Ni, B, B),
        coupling.reshape(Kr, R, Ni, B, B),
        top_rhs,
        top_inverse,
        top_factor,
    )
    return leaf[None, :, None], top


def solution(mesh):
    placed = (
        P("sub", "row", "col", None, None),
        P("sub", "row", "col", None, None),
        P("sub", "row", None, "col", None, None),
        P("sub", "row", None, "col"),
        P(),
        P(),
        P("row", "col", None, None),
    )
    sizes = tuple(mesh.shape[name] for name in ("sub", "row", "col"))
    return jax.shard_map(
        functools.partial(local, sizes),
        mesh=mesh,
        in_specs=placed,
        out_specs=(P("sub", "row", "col", None, None), P("row", None, None)),
        check_vma=False,
    )
```

```python
import functools

import jax
import jax.numpy as jnp
from jax import lax
from jax.experimental import pallas as pl
from jax.experimental.pallas import tpu as pltpu
from jax.sharding import PartitionSpec as P

BF = jnp.bfloat16
F32 = jnp.float32


def dot_nt(a, b):
    return lax.dot_general(a, b, (((1,), (1,)), ((), ())), preferred_element_type=F32)


def dot_nn(a, b):
    return lax.dot_general(a, b, (((1,), (0,)), ((), ())), preferred_element_type=F32)


def lower(block):
    rows = lax.broadcasted_iota(jnp.int32, block.shape, 0)
    cols = lax.broadcasted_iota(jnp.int32, block.shape, 1)
    return jnp.where(rows >= cols, block.astype(F32), 0.0).astype(BF)


def kernel(
    S, R, C,
    pat, rhs_h, linv_h, coup_h, trhs_h, tinv_h, tf_h,
    out, top,
    rhs, ginv, gt, coup, y, u, ub, d1, v, d2, tf, ti, tr, W, FW, res, xf,
    fws, fwr, xs, x, acc, cx, pf, px,
    ld, cp_sem, y_ss, y_rs, tf_ss, tf_rs, d1_ss, d1_rs, d2_ss, d2_rs,
    fw_ss, fw_rs, x1_ss, x1_rs, x2_ss, x2_rs, cx_ss, cx_rs, px_ss, px_rs,
):
    s, r, c = lax.axis_index("sub"), lax.axis_index("row"), lax.axis_index("col")
    Kr, _, Ni, B, _ = coup.shape
    KT, Kc = tf.shape[:2]
    n = y.shape[2]
    ns = n // S
    Kg = min(Kr, Kc)
    chunks = Kr // Kg
    Q = Kc // Kg
    lead = (c * Kc) // Kr
    is_lead = r == lead
    mine = pl.ds(pl.multiple_of(s * ns, ns), ns)

    def remote(src, dst, ss, rs, dev):
        return pltpu.make_async_remote_copy(
            src_ref=src, dst_ref=dst, send_sem=ss, recv_sem=rs,
            device_id=dev, device_id_type=pl.DeviceIdType.MESH,
        )

    def group_of(j):
        return (r * Kr + j * Kg) // Kc

    loads = [
        pltpu.make_async_copy(linv_h, ginv, ld.at[0]),
        pltpu.make_async_copy(rhs_h, rhs, ld.at[1]),
    ]
    for cp in loads:
        cp.start()

    def coup_copy(a, p):
        rr = lax.rem(r + p, R)
        return pltpu.make_async_copy(coup_h.at[a, rr], coup.at[a, rr], cp_sem.at[a, p])

    for j in range(chunks):
        for p in range(R):
            for a in range(j * Kg, (j + 1) * Kg):
                coup_copy(a, p).start()
    ti_copy = pltpu.make_async_copy(tinv_h.at[pl.ds(c * Kc, Kc)], ti, ld.at[2])
    tr_copy = pltpu.make_async_copy(trhs_h.at[pl.ds(c * Kc, Kc), mine], tr, ld.at[3])
    tf_copy = pltpu.make_async_copy(tf_h, tf.at[pl.ds(r * Kr, Kr)], ld.at[4])

    @pl.when(is_lead)
    def _():
        ti_copy.start()
        tr_copy.start()
        tf_copy.start()

    barrier = pltpu.get_barrier_semaphore()
    for p in range(1, S):
        pl.semaphore_signal(
            barrier, inc=1, device_id=(lax.rem(s + p, S), r, c), device_id_type=pl.DeviceIdType.MESH
        )
    for p in range(R):
        for q in range(C):
            if p == 0 and q == 0:
                continue
            pl.semaphore_signal(
                barrier, inc=1, device_id=(s, lax.rem(r + p, R), lax.rem(c + q, C)),
                device_id_type=pl.DeviceIdType.MESH,
            )

    for cp in loads:
        cp.wait()
    for i in range(Ni):
        g = lower(ginv[i])
        gt[i] = g
        y[r, i] = dot_nt(rhs[i], g).astype(BF)

    pl.semaphore_wait(barrier, S - 1 + R * C - 1)

    def y_send(p):
        return remote(y.at[r], y.at[r], y_ss.at[p], y_rs.at[p], (s, lax.rem(r + p, R), c))

    def y_from(p):
        src = lax.rem(r + R - p, R)
        return remote(y.at[src], y.at[src], y_ss.at[p], y_rs.at[p], (s, src, c))

    for p in range(1, R):
        y_send(p).start()

    tf_send = remote(tf_h, tf.at[pl.ds(r * Kr, Kr)], tf_ss, tf_rs.at[r], (s, lead, c))

    @pl.when(r > lead)
    def _():
        tf_send.start()

    def tf_wait(rr):
        remote(tf_h, tf.at[pl.ds(rr * Kr, Kr)], tf_ss, tf_rs.at[rr], (s, lead, c)).wait_recv()

    def add(a, rr, first):
        total = None if first else u[a]
        for i in range(Ni):
            w = pat[a, rr * Ni + i].astype(F32)
            term = dot_nt(y[rr, i], coup[a, rr, i]) * w
            total = term if total is None else total + term
        return total

    def d1_send(j, p):
        to = lax.rem(s + p, S)
        rows = pl.ds(pl.multiple_of(to * ns, ns), ns)
        blocks = pl.ds(j * Kg, Kg)
        return remote(
            ub.at[blocks, rows], d1.at[p, blocks], d1_ss.at[j, p], d1_rs.at[j, p], (to, r, c)
        )

    def d2_send(j):
        g = group_of(j)
        pos = lax.rem(r * Kr + j * Kg, Kc)
        return remote(
            v.at[pl.ds(j * Kg, Kg)], d2.at[c, pl.ds(pos, Kg)], d2_ss.at[j],
            d2_rs.at[pos // Kg, c], (s, (g * Kc) // Kr, g),
        )

    def self_lead(j):
        return jnp.logical_and(is_lead, group_of(j) == c)

    def blk(k):
        return pl.ds(k * B, B)

    def w_row(k):
        g = lower(ti[k])
        W[blk(k), blk(k)] = g
        for b in range(k):
            t = None
            for m in range(b, k):
                term = dot_nn(tf[c * Kc + k, m], W[blk(m), blk(b)])
                t = term if t is None else t + term
            W[blk(k), blk(b)] = (-dot_nn(g, t.astype(BF))).astype(BF)

    def pass_on(j):
        for p in range(1, S):
            d1_send(j, p).wait_recv()
        for b in range(Kg):
            a = j * Kg + b
            total = u[a, mine, :]
            for p in range(1, S):
                total = total + d1[p, a].astype(F32)
            v[a] = total.astype(BF)

        @pl.when(self_lead(j))
        def _():
            d2[c, pl.ds(0, Kg)] = v[pl.ds(j * Kg, Kg)]

        @pl.when(jnp.logical_not(self_lead(j)))
        def _():
            d2_send(j).start()

    for j in range(chunks):
        blocks = range(j * Kg, (j + 1) * Kg)
        for p in range(R):
            if j == 0 and p > 0:
                y_from(R - p).wait_recv()
            for a in blocks:
                coup_copy(a, p).wait()
            for a in blocks:
                total = add(a, lax.rem(r + p, R), p == 0)
                u[a] = total
                if p == R - 1:
                    ub[a] = total.astype(BF)
            if j > 0 and p == 0:
                pass_on(j - 1)
        for t in range(1, S):
            d1_send(j, t).start()
    pass_on(chunks - 1)

    def cx_send(p):
        to = lax.rem(r + p, R)
        return remote(coup_h.at[:, to], cx.at[r], cx_ss.at[p], cx_rs.at[r], (s, to, c))

    def px_send(p):
        to = lax.rem(r + p, R)
        return remote(pf.at[to], px.at[r], px_ss.at[p], px_rs.at[r], (s, to, c))

    cx_own = pltpu.make_async_copy(coup_h.at[:, r], cx.at[r], ld.at[5])
    cx_own.start()
    for p in range(1, R):
        cx_send(p).start()
    for rr in range(R):
        for a in range(Kr):
            for i in range(Ni):
                pf[rr, a, i] = jnp.full((8, B), pat[a, rr * Ni + i].astype(F32))
    px[r] = pf[r]
    for p in range(1, R):
        px_send(p).start()

    def fw_copy(src_c, dst_c):
        return remote(
            fws.at[dst_c], fwr.at[src_c], fw_ss.at[dst_c], fw_rs.at[src_c],
            (s, (dst_c * Kc) // Kr, dst_c),
        )

    def x1_copy(rr, o):
        return remote(
            xs, x.at[pl.ds(c * Kc, Kc), mine], x1_ss.at[rr, o], x1_rs.at[c], (s, rr, o)
        )

    def lead_of(o):
        return (o * Kc) // Kr

    def x2_copy(g, p, rr):
        place = x.at[pl.ds(g * Kc, Kc), mine]
        return remote(
            place, place, x2_ss.at[g, rr, p], x2_rs.at[g, p], (lax.rem(s + p, S), rr, c)
        )

    def x2_each(g, act):
        @pl.when(r == lead_of(g))
        def _():
            for rr in range(R):
                for p in range(S):
                    if p > 0:
                        act(x2_copy(g, p, rr))
                    else:
                        has = jnp.logical_or(rr == r, jnp.logical_and(rr == lead, c < g))

                        @pl.when(jnp.logical_not(has))
                        def _(rr=rr):
                            act(x2_copy(g, 0, rr))

    def x2_forward(g):
        x2_each(g, lambda copy: copy.start())

    def x1_wait(g):
        place = x.at[pl.ds(g * Kc, Kc), mine]
        remote(place, place, x1_ss.at[0, 0], x1_rs.at[g], (s, r, c)).wait_recv()

    @pl.when(is_lead)
    def _():
        ti_copy.wait()
        tf_copy.wait()
        for q in range(1, Q):
            tf_wait(lead + q)
        for k in range(Kc):
            w_row(k)

        def next_products():
            def row(k, carry):
                for b in range(Kc):
                    t = None
                    for m in range(b, Kc):
                        term = dot_nn(tf[(c + 1) * Kc + k, m], W[blk(m), blk(b)])
                        t = term if t is None else t + term
                    FW[pl.ds(pl.multiple_of(k * B, B), B), blk(b)] = t.astype(BF)
                return carry

            lax.fori_loop(0, Kc, row, 0)

        @pl.when(c > 0)
        def _():
            for rr in range(R):
                @pl.when(rr >= lead + Q)
                def _(rr=rr):
                    tf_wait(rr)

        @pl.when(jnp.logical_and(c > 0, c < C - 1))
        def _():
            next_products()

        tr_copy.wait()
        for q in range(Q):
            for o in range(C):
                def take(q=q, o=o):
                    remote(
                        v.at[pl.ds(0, Kg)], d2.at[o, pl.ds(q * Kg, Kg)], d2_ss.at[0],
                        d2_rs.at[q, o], (s, lead + q, o),
                    ).wait_recv()
                if q == 0:
                    pl.when(c != o)(take)
                else:
                    take()
        for k in range(Kc):
            total = tr[k].astype(F32)
            for o in range(C):
                total = total - d2[o, k].astype(F32)
            res[k] = total
        for o in range(C - 1):
            @pl.when(c > o)
            def _(o=o):
                fw_copy(o, c).wait_recv()
                for k in range(Kc):
                    res[k] = res[k] - fwr[o, k].astype(F32)
        rb = [res[k].astype(BF) for k in range(Kc)]

        @pl.when(jnp.logical_and(c > 0, c < C - 1))
        def _():
            for k in range(Kc):
                t = None
                for b in range(Kc):
                    term = dot_nt(rb[b], FW[blk(k), blk(b)])
                    t = term if t is None else t + term
                fws[c + 1, k] = t.astype(BF)
            fw_copy(c, c + 1).start()

        for k in range(Kc):
            t = dot_nt(rb[k], W[blk(k), blk(k)])
            for b in range(k):
                t = t + dot_nt(rb[b], W[blk(k), blk(b)])
            xf[k] = t.astype(BF)

        def give(o):
            for k in range(Kc):
                t = None
                for b in range(Kc):
                    term = dot_nt(xf[b], tf[o * Kc + k, b])
                    t = term if t is None else t + term
                fws[o, k] = t.astype(BF)
            fw_copy(c, o).start()

        @pl.when(c == 0)
        def _():
            for rr in range(R):
                if (rr * Kr) // Kc == 1:
                    tf_wait(rr)
            give(1)
            for rr in range(R):
                if (rr * Kr) // Kc > 1:
                    tf_wait(rr)

        for o in range(2, C):
            @pl.when(c < o - 1)
            def _(o=o):
                give(o)

        @pl.when(c == 0)
        def _():
            next_products()
        for k in range(Kc):
            res[k] = xf[k].astype(F32)
        for o in range(C - 1, 1, -1):
            @pl.when(c < o - 1)
            def _(o=o):
                x1_wait(o)
                for k in range(Kc):
                    t = res[k]
                    for a in range(Kc):
                        t = t - dot_nn(x[o * Kc + a, mine, :], tf[o * Kc + a, k])
                    res[k] = t
                x2_forward(o)
        wb = [res[k].astype(BF) for k in range(Kc)]
        for k in range(Kc):
            t = dot_nn(wb[k], W[blk(k), blk(k)])
            for a in range(k + 1, Kc):
                t = t + dot_nn(wb[a], W[blk(a), blk(k)])
            res[k] = t

        @pl.when(c < C - 1)
        def _():
            x1_wait(c + 1)
            for k in range(Kc):
                t = res[k]
                for a in range(Kc):
                    t = t - dot_nn(x[(c + 1) * Kc + a, mine, :], FW[blk(a), blk(k)])
                res[k] = t
        for k in range(Kc):
            xs[k] = res[k].astype(BF)
        for o in range(C - 2, -1, -1):
            @pl.when(c > o)
            def _(o=o):
                x1_copy(lead_of(o), o).start()
        for o in range(C - 1, -1, -1):
            @pl.when(jnp.logical_and(c != o, jnp.logical_or(c < o, lead_of(o) != lead)))
            def _(o=o):
                x1_copy(lead, o).start()
        for b in range(Kc):
            x[c * Kc + b, mine, :] = xs[b]
        x2_forward(c)

        @pl.when(c < C - 1)
        def _():
            x2_forward(c + 1)

    def x2_from(g, p):
        src = lax.rem(s + S - p, S)
        row = lead_of(g)
        place = x.at[pl.ds(g * Kc, Kc), pl.ds(pl.multiple_of(src * ns, ns), ns)]
        return remote(place, place, x2_ss.at[g, row, p], x2_rs.at[g, p], (src, row, c))

    cx_own.wait()
    for p in range(1, R):
        src = lax.rem(r + p, R)
        remote(coup_h.at[:, r], cx.at[src], cx_ss.at[p], cx_rs.at[src], (s, src, c)).wait_recv()
        remote(pf.at[r], px.at[src], px_ss.at[p], px_rs.at[src], (s, src, c)).wait_recv()

    for g in range(C - 1, -1, -1):
        late = jnp.logical_not(jnp.logical_and(is_lead, c <= g))

        @pl.when(jnp.logical_and(late, r == lead_of(g)))
        def _():
            x1_wait(g)
            x2_forward(g)

        @pl.when(jnp.logical_and(late, r != lead_of(g)))
        def _():
            x2_from(g, 0).wait_recv()

        for p in range(1, S):
            x2_from(g, p).wait_recv()
        for i in range(Ni):
            t = y[r, i].astype(F32) if g == C - 1 else acc[i]
            for b in range(Kc):
                a = g * Kc + b
                owner, at = a // Kr, a % Kr
                t = t - dot_nn(x[a], cx[owner, at, i]) * px[owner, at, i, 0:1, :]
            if g > 0:
                acc[i] = t
            else:
                out[i] = dot_nn(t.astype(BF), gt[i]).astype(BF)
    top[...] = x[pl.ds(r * Kr, Kr)]

    for p in range(1, R):
        y_send(p).wait_send()
        cx_send(p).wait_send()
        px_send(p).wait_send()

    @pl.when(r > lead)
    def _():
        tf_send.wait_send()

    for j in range(chunks):
        for p in range(1, S):
            d1_send(j, p).wait_send()

        @pl.when(jnp.logical_not(self_lead(j)))
        def _():
            d2_send(j).wait_send()

    for g in range(C):
        x2_each(g, lambda copy: copy.wait_send())

    @pl.when(is_lead)
    def _():
        for o in range(C):
            @pl.when(c < o)
            def _(o=o):
                fw_copy(c, o).wait_send()

            @pl.when(jnp.logical_and(c != o, c > o))
            def _(o=o):
                x1_copy(lead_of(o), o).wait_send()

            @pl.when(jnp.logical_and(c != o, jnp.logical_or(c < o, lead_of(o) != lead)))
            def _(o=o):
                x1_copy(lead, o).wait_send()


def local(sizes, leaf_rhs, leaf_inverse, coupling, pattern, top_rhs, top_inverse, top_factor):
    S, R, C = sizes
    _, Kr, NL, _, B, _ = coupling.shape
    Ni = NL // R
    KT, n, _ = top_rhs.shape
    Kc = top_factor.shape[1]
    ns = n // S
    Kg = min(Kr, Kc)
    chunks, Q = Kr // Kg, Kc // Kg
    V = pltpu.VMEM
    D = pltpu.SemaphoreType.DMA
    any_spec = pl.BlockSpec(memory_space=pl.ANY)
    scratch = [
        V((Ni, n, B), BF), V((Ni, B, B), BF), V((Ni, B, B), BF),
        V((Kr, R, Ni, B, B), BF), V((R, Ni, n, B), BF),
        V((Kr, n, B), F32), V((Kr, n, B), BF), V((S, Kr, ns, B), BF), V((Kr, ns, B), BF),
        V((C, Kc, ns, B), BF), V((KT, Kc, B, B), BF), V((Kc, B, B), BF), V((Kc, ns, B), BF),
        V((Kc * B, Kc * B), BF), V((Kc * B, Kc * B), BF), V((Kc, ns, B), F32), V((Kc, ns, B), BF),
        V((C, Kc, ns, B), BF), V((C, Kc, ns, B), BF), V((Kc, ns, B), BF),
        V((KT, n, B), BF), V((Ni, n, B), F32), V((R, Kr, Ni, B, B), BF),
        V((R, Kr, Ni, 8, B), F32), V((R, Kr, Ni, 8, B), F32),
        D((6,)), D((Kr, R)), D((R,)), D((R,)), D, D((R,)),
        D((chunks, S)), D((chunks, S)), D((chunks,)), D((Q, C)),
        D((C,)), D((C,)),
        D((R, C)), D((C,)), D((C, R, S)), D((C, S)), D((R,)), D((R,)), D((R,)), D((R,)),
    ]
    leaf, top = pl.pallas_call(
        functools.partial(kernel, S, R, C),
        out_shape=(
            pltpu.VMEM((Ni, n, B), BF),
            pltpu.VMEM((Kr, n, B), BF),
        ),
        in_specs=[pl.BlockSpec(memory_space=pltpu.SMEM)] + [any_spec] * 6,
        out_specs=(pl.BlockSpec(memory_space=pltpu.VMEM),) * 2,
        scratch_shapes=scratch,
        compiler_params=pltpu.CompilerParams(
            collective_id=0, has_side_effects=True, vmem_limit_bytes=56 * 1024 * 1024
        ),
    )(
        pattern.reshape(Kr, NL),
        leaf_rhs.reshape(Ni, n, B),
        leaf_inverse.reshape(Ni, B, B),
        coupling.reshape(Kr, R, Ni, B, B),
        top_rhs,
        top_inverse,
        top_factor,
    )
    return leaf[None, :, None], top


def solution(mesh):
    placed = (
        P("sub", "row", "col", None, None),
        P("sub", "row", "col", None, None),
        P("sub", "row", None, "col", None, None),
        P("sub", "row", None, "col"),
        P(),
        P(),
        P("row", "col", None, None),
    )
    sizes = tuple(mesh.shape[name] for name in ("sub", "row", "col"))
    return jax.shard_map(
        functools.partial(local, sizes),
        mesh=mesh,
        in_specs=placed,
        out_specs=(P("sub", "row", "col", None, None), P("row", None, None)),
        check_vma=False,
    )
```
